32 devices in a mesh: dp: 2 (over y), tensor: 4 (over z), section: 4 (over x, core).
Axes of the slice: x: 2, y: 2, z: 4, core: 2. Of those that a mesh axis runs over, the one named last changes fastest.
Arguments:
- tokens_in: bfloat16 [5120, 5120], P(('section', 'dp', 'tensor')), parts along dimension 0, may hold values from -4 to 4
- key_cot: bfloat16 [5120, 1024], P(('section', 'dp'), 'tensor'), parts along dimension 0, may hold values from -3 to 3, as said below
- row_mask: int32 [5120], P(('section', 'dp', 'tensor')), parts along dimension 0, may hold values 0 or 1
- w_key: bfloat16 [20480, 1024], P('section', 'tensor'), parts along dimension 0, may hold values from -0.078125 to 0.078125
- momentum: bfloat16 [2, 20480, 1024], P('dp', 'section', 'tensor'), parts along dimension 1, may hold values from -4 to 4
Outputs:
- input_grad: bfloat16 [5120, 5120], P(('section', 'dp', 'tensor')), parts along dimension 0
- new_momentum: bfloat16 [2, 20480, 1024], P('dp', 'section', 'tensor'), parts along dimension 1
- rollout_weight: bfloat16 [4, 20480, 256], P('tensor', 'section'), parts along dimension 1
The draws below stay inside these ranges and needn't reach their ends.
There are 4 independent parts, one for each index of `section`. The reference program is written for one: setup_inputs(seed, part) draws one part's arguments, and reference() takes and returns one part's arrays. A program takes and returns all parts, laid end to end along the dimension named above; each array names one. Nothing has to cross between parts.
Inputs may be any that keep to these rules, and one draw needn't show every extreme that they name: `key_cot`: every entry is a multiple of 0.125.
All inputs are finite; a program needn't handle non-finite values. No bound on the sum of `row_mask` on one device may be relied on, other than what follows from the above.
Results may differ from the reference program's by a relative error of at most 0.017.
Values may be sent and summed in bfloat16 or wider, within the bound.
A program may use at most 128 MiB of HBM per device.

```python
import jax
import jax.numpy as jnp
from jax import lax

D = 5120
KV = 1024
SEQ_ROWS = 640
ROWS = 1280
N_DP = 2
N_TENSOR = 4


def eighths(key, shape, reach):
    uniform_part = jax.random.uniform(key, shape, jnp.float32)
    return (jnp.floor(uniform_part * (2.0 * reach + 1.0)) - reach) / 8.0


def on_grid(values, quantum):
    stored = lax.optimization_barrier(values.astype(jnp.bfloat16)).astype(jnp.float32)
    return (jnp.floor(stored / quantum) * quantum).astype(jnp.bfloat16)


def draw_tokens_in(key, part):
    key = jax.random.fold_in(key, 11)
    longer = max(0, (SEQ_ROWS - 1).bit_length() - 10)
    quantum = 2.0 ** ((longer + 1) // 2 - 11)
    values = jnp.clip(jax.random.normal(key, (ROWS, D), jnp.float32), -4.0, 4.0)
    return on_grid(values, quantum)


def draw_key_cot(key, part):
    key = jax.random.fold_in(key, 23)
    values = eighths(key, (ROWS, KV), 16.0)
    return values.astype(jnp.bfloat16)


def plant(array, rng, smallest, top_value):
    spot = [jax.random.randint(jax.random.fold_in(rng, axis), (), 0, length) for axis, length in enumerate(array.shape)]
    widest = array.shape.index(max(array.shape))
    next_to = spot[:widest] + [(spot[widest] + 1) % array.shape[widest]] + spot[widest + 1:]
    return array.at[tuple(spot)].set(smallest).at[tuple(next_to)].set(top_value)


def shard_levels(key, dims, pieces, least, largest):
    def one(dim, blocks):
        draws = jax.random.uniform(jax.random.fold_in(jax.random.fold_in(key, 6), dim), (blocks,), jnp.float32, least / len(pieces), largest / len(pieces))
        return jnp.repeat(jnp.exp(draws), dims[dim] // blocks).reshape((-1,) + (1,) * (len(dims) - dim - 1))

    loudness = one(*pieces[0])
    for cut in pieces[1:]:
        loudness = loudness * one(*cut)
    return loudness


def noise(key, shape, spread, limit, shards=(), kind=jnp.bfloat16):
    entries = spread * jax.random.normal(key, shape, jnp.float32)
    if shards:
        entries = entries * shard_levels(key, shape, shards, -0.22, 0.18)
    return jnp.clip(entries, -limit, limit).astype(kind)


def setup_inputs(seed: int = 0, part: int = 0) -> dict:
    streams_of = jax.random.split(jax.random.key(seed), 6)
    part_keys = jax.random.split(jax.random.fold_in(streams_of[5], part), 6)
    tokens_in = draw_tokens_in(jax.random.fold_in(jax.random.fold_in(streams_of[5], part), 71), part)
    key_cot = draw_key_cot(jax.random.fold_in(jax.random.fold_in(streams_of[5], part), 71), part)
    row_mask = plant((jax.random.randint(part_keys[2], (ROWS,), 0, 4) < 3).astype(jnp.int32), jax.random.fold_in(part_keys[2], 1), 0, 1)
    w_key = noise(part_keys[3], (D, KV), D ** -0.5, 0.078125, ((1, 4),))
    momentum = noise(part_keys[4], (N_DP, D, KV), 0.5, 4.0, ((0, 2), (2, 4)))
    return {"tokens_in": tokens_in, "key_cot": key_cot, "row_mask": row_mask, "w_key": w_key, "momentum": momentum}


beta_slow = 0.99
beta_vote = 0.9
step_rate = 0.02


def reference(tokens_in, key_cot, row_mask, w_key, momentum):
    mask_half = row_mask.astype(jnp.bfloat16)[:, None]
    masked_cot = key_cot * mask_half

    def worker(worker_id):
        offset = worker_id * SEQ_ROWS
        token_block = lax.dynamic_slice_in_dim(tokens_in, offset, SEQ_ROWS, 0)
        cot_block = lax.dynamic_slice_in_dim(masked_cot, offset, SEQ_ROWS, 0)
        return lax.dot_general(token_block, cot_block, (((0,), (0,)), ((), ())), preferred_element_type=jnp.float32)

    key_grad = lax.map(worker, jnp.arange(N_DP, dtype=jnp.int32))
    prior = momentum.astype(jnp.float32)
    new_momentum = (beta_slow * prior + (1.0 - beta_slow) * key_grad).astype(jnp.bfloat16)
    interp = beta_vote * prior + (1.0 - beta_vote) * key_grad
    vote_count = jnp.sum((interp > 0).astype(jnp.int32), axis=0, dtype=jnp.int32)
    direction = jnp.sign((2 * vote_count - N_DP).astype(jnp.float32))
    updated = (w_key.astype(jnp.float32) - step_rate * direction).astype(jnp.bfloat16)
    blocks = updated.reshape(D, 4, KV // 4).transpose(1, 0, 2)
    rollout_weight = jnp.repeat(blocks, N_TENSOR // 4, axis=0)
    head_width = KV // N_TENSOR

    def head_group(running, group_id):
        cot_cols = lax.dynamic_slice_in_dim(key_cot, group_id * head_width, head_width, 1)
        weight_cols = lax.dynamic_slice_in_dim(w_key, group_id * head_width, head_width, 1)
        partial_term = lax.dot_general(cot_cols, weight_cols, (((1,), (1,)), ((), ())), preferred_element_type=jnp.float32).astype(jnp.bfloat16)
        return running + partial_term.astype(jnp.float32), None

    summed, _ = lax.scan(head_group, jnp.zeros((ROWS, D), jnp.float32), jnp.arange(N_TENSOR, dtype=jnp.int32))
    input_grad = (summed * row_mask.astype(jnp.float32)[:, None]).astype(jnp.bfloat16)
    return (input_grad, new_momentum, rollout_weight)
```

```python
import functools

import jax
import jax.numpy as jnp
from jax import lax
from jax.experimental import pallas as pl
from jax.experimental.pallas import tpu as pltpu
from jax.sharding import PartitionSpec as P

beta_slow = 0.99
beta_vote = 0.9
step_rate = 0.02
MESH = pl.DeviceIdType.MESH


def swapped(array, axis, stride):
    return lax.ppermute(array, axis, [(i, i ^ 1 << stride) for i in range(lax.axis_size(axis))])


def line_kernel(
    n, workers, chunks, sub,
    tok_ref, cot_ref, mask_ref, w_ref, mom_ref,
    grad_out, mom_out, upd_out,
    gathered, sums, last_sum, total, grad_buf, mom_buf, upd_buf, votes,
    send_sem, recv_sem, vote_send, vote_recv, out_sem,
):
    z = lax.axis_index("tensor")
    worker = lax.axis_index("dp")
    rows = tok_ref.shape[0]
    width = tok_ref.shape[1] // chunks
    words = sub // 32

    barrier = pltpu.get_barrier_semaphore()

    @pl.when(z > 0)
    def _():
        pl.semaphore_signal(barrier, inc=1, device_id={"tensor": z - 1}, device_id_type=MESH)

    @pl.when(z < n - 1)
    def _():
        pl.semaphore_signal(barrier, inc=1, device_id={"tensor": z + 1}, device_id_type=MESH)

    for step in range(1, workers):
        pl.semaphore_signal(
            barrier, inc=1, device_id={"dp": lax.rem(worker + step, workers)}, device_id_type=MESH
        )

    @pl.when(jnp.logical_and(z > 0, z < n - 1))
    def _():
        pl.semaphore_wait(barrier, workers + 1)

    @pl.when(jnp.logical_or(z == 0, z == n - 1))
    def _():
        pl.semaphore_wait(barrier, workers)

    places = (z, n - 1 - z)

    def named(way, index):
        return index if way == 0 else n - 1 - index

    def block(index):
        return pl.ds(pl.multiple_of(index * rows, rows), rows)

    def columns(j):
        return pl.ds(pl.multiple_of(j * width, width), width)

    def hop(way, j, k, src, dst):
        return pltpu.make_async_remote_copy(
            src_ref=src,
            dst_ref=dst,
            send_sem=send_sem.at[way, j, k],
            recv_sem=recv_sem.at[way, j, k],
            device_id={"tensor": z + 1 if way == 0 else z - 1},
            device_id_type=MESH,
        )

    def any_hop(way, j, k):
        return hop(way, j, k, last_sum.at[j], last_sum.at[j])

    def term(j, d):
        return lax.dot_general(
            cot_ref[block(d), :], w_ref[columns(j), :],
            (((1,), (1,)), ((), ())), preferred_element_type=jnp.float32,
        )

    def send_tokens(way, j, k, shard):
        piece = gathered.at[j, block(shard)]
        hop(way, j, k, piece, piece).start()

    def send_own(j):
        gathered[j, block(z)] = (
            tok_ref[:, columns(j)].astype(jnp.float32) * mask_ref[...]
        ).astype(jnp.bfloat16)
        for way in range(2):
            @pl.when(places[way] < n - 1)
            def _():
                send_tokens(way, j, 0, z)

    def slot(j, k):
        for way in range(2):
            place = places[way]

            @pl.when(place > 0)
            def _():
                any_hop(way, j, k).wait_recv()

            @pl.when(jnp.logical_and(k + 1 <= place, place < n - 1))
            def _():
                send_tokens(way, j, k + 1, named(way, place - 1 - k))

            @pl.when(k + 1 > place)
            def _():
                d = named(way, n + place - k - 1)
                total[...] = term(j, d)

                @pl.when(place > 0)
                def _():
                    total[...] += sums[j, d].astype(jnp.float32)

                sums[j, d] = total[...].astype(jnp.bfloat16)
                src = sums.at[j, d]
                dst = last_sum.at[j] if way == 1 and k + 1 == n - 1 else src
                hop(way, j, k + 1, src, dst).start()

    def vote_copy(j, step, source):
        piece = votes.at[source, j]
        return pltpu.make_async_remote_copy(
            src_ref=piece,
            dst_ref=piece,
            send_sem=vote_send.at[step, j],
            recv_sem=vote_recv.at[step, j],
            device_id={"dp": lax.rem(worker + step, workers)},
            device_id_type=MESH,
        )

    def momentum_step(j):
        def part(i, carry):
            at = pl.ds(pl.multiple_of(j * width + i * sub, sub), sub)
            key_grad = lax.dot_general(
                gathered[j, :, pl.ds(pl.multiple_of(i * sub, sub), sub)], cot_ref[...],
                (((0,), (0,)), ((), ())), preferred_element_type=jnp.float32,
            )
            prior = mom_ref[at, :].astype(jnp.float32)
            mom_buf[at, :] = (beta_slow * prior + (1.0 - beta_slow) * key_grad).astype(jnp.bfloat16)
            interp = beta_vote * prior + (1.0 - beta_vote) * key_grad
            positive = (interp > 0).astype(jnp.int32)
            packed = positive[:words]
            for bit in range(1, 32):
                packed = packed | (positive[bit * words : (bit + 1) * words] << bit)
            votes[worker, j, pl.ds(pl.multiple_of(i * words, words), words)] = packed
            return carry

        lax.fori_loop(0, width // sub, part, 0)
        for step in range(1, workers):
            vote_copy(j, step, worker).start()
        pltpu.make_async_copy(
            mom_buf.at[columns(j)], mom_out.at[columns(j)], out_sem.at[0, j]
        ).start()

    def weight_step(j):
        for step in range(1, workers):
            vote_copy(j, step, worker).wait_recv()

        def part(i, carry):
            held = [
                votes[r, j, pl.ds(pl.multiple_of(i * words, words), words)] for r in range(workers)
            ]
            directions = []
            for bit in range(32):
                count = sum(((h >> bit) & 1) for h in held)
                twice = 2 * count - workers
                directions.append(jnp.minimum(jnp.maximum(twice, -1), 1))
            direction = jnp.concatenate(directions, 0).astype(jnp.float32)
            at = pl.ds(pl.multiple_of(j * width + i * sub, sub), sub)
            upd_buf[at, :] = (w_ref[at, :].astype(jnp.float32) - step_rate * direction).astype(
                jnp.bfloat16
            )
            return carry

        lax.fori_loop(0, width // sub, part, 0)
        pltpu.make_async_copy(
            upd_buf.at[columns(j)], upd_out.at[columns(j)], out_sem.at[1, j]
        ).start()

    def finish_grad(j):
        total[...] = term(j, z)
        for way in range(2):
            @pl.when(places[way] > 0)
            def _():
                any_hop(way, j, n - 1).wait_recv()
                came = sums[j, z] if way == 0 else last_sum[j]
                total[...] += came.astype(jnp.float32)

        grad_buf[j] = (total[...] * mask_ref[...]).astype(jnp.bfloat16)
        pltpu.make_async_copy(
            grad_buf.at[j], grad_out.at[:, columns(j)], out_sem.at[2, j]
        ).start()

    send_own(0)

    def one_chunk(j, carry):
        for k in range(n - 1):
            slot(j, k)
            if k == 0:
                @pl.when(j + 1 < chunks)
                def _():
                    send_own(j + 1)

        momentum_step(j)

        @pl.when(j > 0)
        def _():
            weight_step(j - 1)

        finish_grad(j)
        return carry

    lax.fori_loop(0, chunks, one_chunk, 0)
    weight_step(chunks - 1)

    def drain(j, carry):
        for way in range(2):
            @pl.when(places[way] < n - 1)
            def _():
                for k in range(n):
                    any_hop(way, j, k).wait_send()
        for step in range(1, workers):
            vote_copy(j, step, worker).wait_send()
        pltpu.make_async_copy(
            mom_buf.at[columns(j)], mom_out.at[columns(j)], out_sem.at[0, j]
        ).wait()
        pltpu.make_async_copy(
            upd_buf.at[columns(j)], upd_out.at[columns(j)], out_sem.at[1, j]
        ).wait()
        pltpu.make_async_copy(
            grad_buf.at[j], grad_out.at[:, columns(j)], out_sem.at[2, j]
        ).wait()
        return carry

    lax.fori_loop(0, chunks, drain, 0)


def per_device(tokens_in, key_cot, row_mask, w_key, momentum):
    rows, features = tokens_in.shape
    head_cols = w_key.shape[1]
    n = lax.axis_size("tensor")
    workers = lax.axis_size("dp")
    sub = 256
    chunks = 5
    width = features // chunks
    bf16 = jnp.bfloat16
    vmem = pl.BlockSpec(memory_space=pltpu.VMEM)
    hbm = pl.BlockSpec(memory_space=pl.ANY)
    dma = pltpu.SemaphoreType.DMA
    input_grad, new_momentum, updated = pl.pallas_call(
        functools.partial(line_kernel, n, workers, chunks, sub),
        out_shape=(
            jax.ShapeDtypeStruct((rows, features), bf16),
            jax.ShapeDtypeStruct((features, head_cols), bf16),
            jax.ShapeDtypeStruct((features, head_cols), bf16),
        ),
        in_specs=[vmem] * 5,
        out_specs=(hbm, hbm, hbm),
        scratch_shapes=[
            pltpu.VMEM((chunks, n * rows, width), bf16),
            pltpu.VMEM((chunks, n, rows, width), bf16),
            pltpu.VMEM((chunks, rows, width), bf16),
            pltpu.VMEM((rows, width), jnp.float32),
            pltpu.VMEM((chunks, rows, width), bf16),
            pltpu.VMEM((features, head_cols), bf16),
            pltpu.VMEM((features, head_cols), bf16),
            pltpu.VMEM((workers, chunks, width // 32, head_cols), jnp.int32),
            dma((2, chunks, n)),
            dma((2, chunks, n)),
            dma((workers, chunks)),
            dma((workers, chunks)),
            dma((3, chunks)),
        ],
        compiler_params=pltpu.CompilerParams(
            collective_id=0, has_side_effects=True, vmem_limit_bytes=56 * 2**20
        ),
        cost_estimate=pl.CostEstimate(
            flops=4 * n * rows * features * head_cols,
            bytes_accessed=2 * (2 * rows * features + 4 * features * head_cols),
            transcendentals=0,
        ),
    )(tokens_in, key_cot, row_mask.astype(jnp.float32)[:, None], w_key, momentum[0])
    column_block = updated
    position = lax.axis_index("tensor")
    for depth_bit in range((n // 4).bit_length() - 1):
        partner = swapped(column_block, "tensor", depth_bit)
        lower_half = jnp.bitwise_and(jnp.right_shift(position, depth_bit), 1) == 0
        column_block = jnp.where(
            lower_half,
            jnp.concatenate([column_block, partner], 1),
            jnp.concatenate([partner, column_block], 1),
        )
    return (input_grad, new_momentum[None], column_block[None])


def solution(mesh):
    return jax.shard_map(
        per_device,
        mesh=mesh,
        in_specs=(
            P(("section", "dp", "tensor"), None),
            P(("section", "dp"), "tensor"),
            P(("section", "dp", "tensor")),
            P("section", "tensor"),
            P("dp", "section", "tensor"),
        ),
        out_specs=(
            P(("section", "dp", "tensor"), None),
            P("dp", "section", "tensor"),
            P("tensor", "section", None),
        ),
        check_vma=False,
    )
```

```python
import functools

import jax
import jax.numpy as jnp
from jax import lax
from jax.experimental import pallas as pl
from jax.experimental.pallas import tpu as pltpu
from jax.sharding import PartitionSpec as P

beta_slow = 0.99
beta_vote = 0.9
step_rate = 0.02
MESH = pl.DeviceIdType.MESH


def swapped(array, axis, stride):
    return lax.ppermute(array, axis, [(i, i ^ 1 << stride) for i in range(lax.axis_size(axis))])


def line_kernel(
    n, workers, chunks, lanes, sub,
    tok_in, cot_in, mask_ref, w_in, mom_in,
    grad_out, mom_out, upd_out,
    tok_ref, cot_ref, w_ref, mom_ref,
    gathered, sums, last_sum, total, grad_buf, mom_buf, upd_buf, votes,
    send_sem, recv_sem, vote_send, vote_recv, out_sem, in_sem,
):
    z = lax.axis_index("tensor")
    worker = lax.axis_index("dp")
    loads = [
        pltpu.make_async_copy(src, dst, in_sem.at[i])
        for i, (src, dst) in enumerate(
            ((tok_in, tok_ref), (cot_in, cot_ref), (w_in, w_ref), (mom_in, mom_ref))
        )
    ]
    for load in loads:
        load.start()
    rows = tok_ref.shape[0]
    width = tok_ref.shape[1] // chunks
    words = sub // 32

    barrier = pltpu.get_barrier_semaphore()

    @pl.when(z > 0)
    def _():
        pl.semaphore_signal(barrier, inc=1, device_id={"tensor": z - 1}, device_id_type=MESH)

    @pl.when(z < n - 1)
    def _():
        pl.semaphore_signal(barrier, inc=1, device_id={"tensor": z + 1}, device_id_type=MESH)

    for step in range(1, workers):
        pl.semaphore_signal(
            barrier, inc=1, device_id={"dp": lax.rem(worker + step, workers)}, device_id_type=MESH
        )

    @pl.when(jnp.logical_and(z > 0, z < n - 1))
    def _():
        pl.semaphore_wait(barrier, workers + 1)

    @pl.when(jnp.logical_or(z == 0, z == n - 1))
    def _():
        pl.semaphore_wait(barrier, workers)

    places = (z, n - 1 - z)

    def named(way, index):
        return index if way == 0 else n - 1 - index

    def block(index):
        return pl.ds(pl.multiple_of(index * rows, rows), rows)

    def columns(j):
        return pl.ds(pl.multiple_of(j * width, width), width)

    def hop(way, j, k, src, dst):
        return pltpu.make_async_remote_copy(
            src_ref=src,
            dst_ref=dst,
            send_sem=send_sem.at[way, j, k],
            recv_sem=recv_sem.at[way, j, k],
            device_id={"tensor": z + 1 if way == 0 else z - 1},
            device_id_type=MESH,
        )

    def any_hop(way, j, k):
        return hop(way, j, k, last_sum.at[j], last_sum.at[j])

    def term(j, d):
        return lax.dot_general(
            cot_ref[block(d), :], w_ref[columns(j), :],
            (((1,), (1,)), ((), ())), preferred_element_type=jnp.float32,
        )

    def send_tokens(way, j, k, shard):
        piece = gathered.at[j, block(shard)]
        hop(way, j, k, piece, piece).start()

    def send_own(j):
        gathered[j, block(z)] = (
            tok_ref[:, columns(j)].astype(jnp.float32) * mask_ref[...]
        ).astype(jnp.bfloat16)
        for way in range(2):
            @pl.when(places[way] < n - 1)
            def _():
                send_tokens(way, j, 0, z)

    def slot(j, k):
        for way in range(2):
            place = places[way]

            @pl.when(place > 0)
            def _():
                any_hop(way, j, k).wait_recv()

            @pl.when(jnp.logical_and(k + 1 <= place, place < n - 1))
            def _():
                send_tokens(way, j, k + 1, named(way, place - 1 - k))

            @pl.when(k + 1 > place)
            def _():
                d = named(way, n + place - k - 1)
                total[...] = term(j, d)

                @pl.when(place > 0)
                def _():
                    total[...] += sums[j, d].astype(jnp.float32)

                sums[j, d] = total[...].astype(jnp.bfloat16)
                src = sums.at[j, d]
                dst = last_sum.at[j] if way == 1 and k + 1 == n - 1 else src
                hop(way, j, k + 1, src, dst).start()

    def vote_copy(j, step, source):
        piece = votes.at[source, j]
        return pltpu.make_async_remote_copy(
            src_ref=piece,
            dst_ref=piece,
            send_sem=vote_send.at[step, j],
            recv_sem=vote_recv.at[step, j],
            device_id={"dp": lax.rem(worker + step, workers)},
            device_id_type=MESH,
        )

    def momentum_step(j):
        def part(i, carry):
            at = pl.ds(pl.multiple_of(j * width + i * sub, sub), sub)
            key_grad = lax.dot_general(
                gathered[j, :, pl.ds(pl.multiple_of(i * sub, sub), sub)], cot_ref[...],
                (((0,), (0,)), ((), ())), preferred_element_type=jnp.float32,
            )
            prior = mom_ref[at, :].astype(jnp.float32)
            mom_buf[at, :] = (beta_slow * prior + (1.0 - beta_slow) * key_grad).astype(jnp.bfloat16)
            interp = beta_vote * prior + (1.0 - beta_vote) * key_grad
            positive = (interp > 0).astype(jnp.int32)
            packed = positive[:words]
            for bit in range(1, 32):
                packed = packed | (positive[bit * words : (bit + 1) * words] << bit)
            votes[worker, j, pl.ds(pl.multiple_of(i * words, words), words)] = packed
            return carry

        lax.fori_loop(0, width // sub, part, 0)
        for step in range(1, workers):
            vote_copy(j, step, worker).start()
        pltpu.make_async_copy(
            mom_buf.at[columns(j)], mom_out.at[columns(j)], out_sem.at[0, j]
        ).start()

    def weight_step(j):
        for step in range(1, workers):
            vote_copy(j, step, worker).wait_recv()

        def part(i, carry):
            held = [
                votes[r, j, pl.ds(pl.multiple_of(i * words, words), words)] for r in range(workers)
            ]
            directions = []
            for bit in range(32):
                count = sum(((h >> bit) & 1) for h in held)
                twice = 2 * count - workers
                directions.append(jnp.minimum(jnp.maximum(twice, -1), 1))
            direction = jnp.concatenate(directions, 0).astype(jnp.float32)
            at = pl.ds(pl.multiple_of(j * width + i * sub, sub), sub)
            upd_buf[at, :] = (w_ref[at, :].astype(jnp.float32) - step_rate * direction).astype(
                jnp.bfloat16
            )
            return carry

        lax.fori_loop(0, width // sub, part, 0)
        pltpu.make_async_copy(
            upd_buf.at[columns(j)], upd_out.at[columns(j)], out_sem.at[1, j]
        ).start()

    def finish_grad(j):
        total[...] = term(j, z)
        for way in range(2):
            @pl.when(places[way] > 0)
            def _():
                any_hop(way, j, n - 1).wait_recv()
                came = sums[j, z] if way == 0 else last_sum[j]
                total[...] += came.astype(jnp.float32)

        grad_buf[j] = (total[...] * mask_ref[...]).astype(jnp.bfloat16)
        pltpu.make_async_copy(
            grad_buf.at[j], grad_out.at[:, columns(j)], out_sem.at[2, j]
        ).start()

    def each(function, group):
        def one(half, carry):
            function(group * lanes + half)
            return carry

        lax.fori_loop(0, lanes, one, 0)

    groups = chunks // lanes
    loads[0].wait()
    each(send_own, 0)
    for load in loads[1:]:
        load.wait()

    def one_group(group, carry):
        for k in range(n - 1):
            each(lambda j: slot(j, k), group)
            if k == 0:
                @pl.when(group + 1 < groups)
                def _():
                    each(send_own, group + 1)

                @pl.when(group > 0)
                def _():
                    each(momentum_step, group - 1)

                @pl.when(group > 1)
                def _():
                    each(weight_step, group - 2)

                @pl.when(group > 0)
                def _():
                    each(finish_grad, group - 1)

        return carry

    lax.fori_loop(0, groups, one_group, 0)
    each(momentum_step, groups - 1)
    if groups > 1:
        each(weight_step, groups - 2)
    each(weight_step, groups - 1)
    each(finish_grad, groups - 1)

    def drain(j, carry):
        for way in range(2):
            @pl.when(places[way] < n - 1)
            def _():
                for k in range(n):
                    any_hop(way, j, k).wait_send()
        for step in range(1, workers):
            vote_copy(j, step, worker).wait_send()
        pltpu.make_async_copy(
            mom_buf.at[columns(j)], mom_out.at[columns(j)], out_sem.at[0, j]
        ).wait()
        pltpu.make_async_copy(
            upd_buf.at[columns(j)], upd_out.at[columns(j)], out_sem.at[1, j]
        ).wait()
        pltpu.make_async_copy(
            grad_buf.at[j], grad_out.at[:, columns(j)], out_sem.at[2, j]
        ).wait()
        return carry

    lax.fori_loop(0, chunks, drain, 0)


def per_device(tokens_in, key_cot, row_mask, w_key, momentum):
    rows, features = tokens_in.shape
    head_cols = w_key.shape[1]
    n = lax.axis_size("tensor")
    workers = lax.axis_size("dp")
    sub = 256
    chunks = 10
    lanes = 2
    width = features // chunks
    bf16 = jnp.bfloat16
    vmem = pl.BlockSpec(memory_space=pltpu.VMEM)
    hbm = pl.BlockSpec(memory_space=pl.ANY)
    dma = pltpu.SemaphoreType.DMA
    input_grad, new_momentum, updated = pl.pallas_call(
        functools.partial(line_kernel, n, workers, chunks, lanes, sub),
        out_shape=(
            jax.ShapeDtypeStruct((rows, features), bf16),
            jax.ShapeDtypeStruct((features, head_cols), bf16),
            jax.ShapeDtypeStruct((features, head_cols), bf16),
        ),
        in_specs=[hbm, hbm, vmem, hbm, hbm],
        out_specs=(hbm, hbm, hbm),
        scratch_shapes=[
            pltpu.VMEM((rows, features), bf16),
            pltpu.VMEM(key_cot.shape, bf16),
            pltpu.VMEM((features, head_cols), bf16),
            pltpu.VMEM((features, head_cols), bf16),
            pltpu.VMEM((chunks, n * rows, width), bf16),
            pltpu.VMEM((chunks, n, rows, width), bf16),
            pltpu.VMEM((chunks, rows, width), bf16),
            pltpu.VMEM((rows, width), jnp.float32),
            pltpu.VMEM((chunks, rows, width), bf16),
            pltpu.VMEM((features, head_cols), bf16),
            pltpu.VMEM((features, head_cols), bf16),
            pltpu.VMEM((workers, chunks, width // 32, head_cols), jnp.int32),
            dma((2, chunks, n)),
            dma((2, chunks, n)),
            dma((workers, chunks)),
            dma((workers, chunks)),
            dma((3, chunks)),
            dma((4,)),
        ],
        compiler_params=pltpu.CompilerParams(
            collective_id=0, has_side_effects=True, vmem_limit_bytes=56 * 2**20
        ),
        cost_estimate=pl.CostEstimate(
            flops=4 * n * rows * features * head_cols,
            bytes_accessed=2 * (2 * rows * features + 4 * features * head_cols),
            transcendentals=0,
        ),
    )(tokens_in, key_cot, row_mask.astype(jnp.float32)[:, None], w_key, momentum[0])
    column_block = updated
    position = lax.axis_index("tensor")
    for depth_bit in range((n // 4).bit_length() - 1):
        partner = swapped(column_block, "tensor", depth_bit)
        lower_half = jnp.bitwise_and(jnp.right_shift(position, depth_bit), 1) == 0
        column_block = jnp.where(
            lower_half,
            jnp.concatenate([column_block, partner], 1),
            jnp.concatenate([partner, column_block], 1),
        )
    return (input_grad, new_momentum[None], column_block[None])


def solution(mesh):
    return jax.shard_map(
        per_device,
        mesh=mesh,
        in_specs=(
            P(("section", "dp", "tensor"), None),
            P(("section", "dp"), "tensor"),
            P(("section", "dp", "tensor")),
            P("section", "tensor"),
            P("dp", "section", "tensor"),
        ),
        out_specs=(
            P(("section", "dp", "tensor"), None),
            P("dp", "section", "tensor"),
            P("tensor", "section", None),
        ),
        check_vma=False,
    )
```

```python
import functools

import jax
import jax.numpy as jnp
from jax import lax
from jax.experimental import pallas as pl
from jax.experimental.pallas import tpu as pltpu
from jax.sharding import PartitionSpec as P

beta_slow = 0.99
beta_vote = 0.9
step_rate = 0.02
MESH = pl.DeviceIdType.MESH


def swapped(array, axis, stride):
    return lax.ppermute(array, axis, [(i, i ^ 1 << stride) for i in range(lax.axis_size(axis))])


def line_kernel(
    n, workers, chunks, lanes, sub,
    tok_in, cot_in, mask_ref, w_in, mom_in,
    grad_out, mom_out, upd_out,
    tok_ref, cot_ref, w_ref, mom_ref,
    gathered, sums, last_sum, total, votes,
    send_sem, recv_sem, vote_send, vote_recv, in_sem,
):
    z = lax.axis_index("tensor")
    worker = lax.axis_index("dp")
    loads = [
        pltpu.make_async_copy(src, dst, in_sem.at[i])
        for i, (src, dst) in enumerate(
            ((tok_in, tok_ref), (cot_in, cot_ref), (w_in, w_ref), (mom_in, mom_ref))
        )
    ]
    for load in loads:
        load.start()
    rows = tok_ref.shape[0]
    width = tok_ref.shape[1] // chunks
    words = sub // 32

    barrier = pltpu.get_barrier_semaphore()

    @pl.when(z > 0)
    def _():
        pl.semaphore_signal(barrier, inc=1, device_id={"tensor": z - 1}, device_id_type=MESH)

    @pl.when(z < n - 1)
    def _():
        pl.semaphore_signal(barrier, inc=1, device_id={"tensor": z + 1}, device_id_type=MESH)

    for step in range(1, workers):
        pl.semaphore_signal(
            barrier, inc=1, device_id={"dp": lax.rem(worker + step, workers)}, device_id_type=MESH
        )

    @pl.when(jnp.logical_and(z > 0, z < n - 1))
    def _():
        pl.semaphore_wait(barrier, workers + 1)

    @pl.when(jnp.logical_or(z == 0, z == n - 1))
    def _():
        pl.semaphore_wait(barrier, workers)

    places = (z, n - 1 - z)

    def named(way, index):
        return index if way == 0 else n - 1 - index

    def block(index):
        return pl.ds(pl.multiple_of(index * rows, rows), rows)

    def columns(j):
        return pl.ds(pl.multiple_of(j * width, width), width)

    def hop(way, j, k, src, dst):
        return pltpu.make_async_remote_copy(
            src_ref=src,
            dst_ref=dst,
            send_sem=send_sem.at[way, j, k],
            recv_sem=recv_sem.at[way, j, k],
            device_id={"tensor": z + 1 if way == 0 else z - 1},
            device_id_type=MESH,
        )

    def any_hop(way, j, k):
        return hop(way, j, k, last_sum.at[j], last_sum.at[j])

    def term(j, d):
        return lax.dot_general(
            cot_ref[block(d), :], w_ref[columns(j), :],
            (((1,), (1,)), ((), ())), preferred_element_type=jnp.float32,
        )

    def send_tokens(way, j, k, shard):
        piece = gathered.at[j, block(shard)]
        hop(way, j, k, piece, piece).start()

    def send_own(j):
        gathered[j, block(z)] = (
            tok_ref[:, columns(j)].astype(jnp.float32) * mask_ref[...]
        ).astype(jnp.bfloat16)
        for way in range(2):
            @pl.when(places[way] < n - 1)
            def _():
                send_tokens(way, j, 0, z)

    def slot(j, k):
        for way in range(2):
            place = places[way]

            @pl.when(place > 0)
            def _():
                any_hop(way, j, k).wait_recv()

            @pl.when(jnp.logical_and(k + 1 <= place, place < n - 1))
            def _():
                send_tokens(way, j, k + 1, named(way, place - 1 - k))

            @pl.when(k + 1 > place)
            def _():
                d = named(way, n + place - k - 1)
                total[...] = term(j, d)

                @pl.when(place > 0)
                def _():
                    total[...] += sums[j, d].astype(jnp.float32)

                sums[j, d] = total[...].astype(jnp.bfloat16)
                src = sums.at[j, d]
                dst = last_sum.at[j] if way == 1 and k + 1 == n - 1 else src
                hop(way, j, k + 1, src, dst).start()

    def vote_copy(j, step, source):
        piece = votes.at[source, j]
        return pltpu.make_async_remote_copy(
            src_ref=piece,
            dst_ref=piece,
            send_sem=vote_send.at[step, j],
            recv_sem=vote_recv.at[step, j],
            device_id={"dp": lax.rem(worker + step, workers)},
            device_id_type=MESH,
        )

    def momentum_step(j):
        def part(i, carry):
            at = pl.ds(pl.multiple_of(j * width + i * sub, sub), sub)
            key_grad = lax.dot_general(
                gathered[j, :, pl.ds(pl.multiple_of(i * sub, sub), sub)], cot_ref[...],
                (((0,), (0,)), ((), ())), preferred_element_type=jnp.float32,
            )
            prior = mom_ref[at, :].astype(jnp.float32)
            mom_out[at, :] = (beta_slow * prior + (1.0 - beta_slow) * key_grad).astype(jnp.bfloat16)
            interp = beta_vote * prior + (1.0 - beta_vote) * key_grad
            positive = (interp > 0).astype(jnp.int32)
            packed = positive[:words]
            for bit in range(1, 32):
                packed = packed | (positive[bit * words : (bit + 1) * words] << bit)
            votes[worker, j, pl.ds(pl.multiple_of(i * words, words), words)] = packed
            return carry

        lax.fori_loop(0, width // sub, part, 0)
        for step in range(1, workers):
            vote_copy(j, step, worker).start()

    def weight_step(j):
        for step in range(1, workers):
            vote_copy(j, step, worker).wait_recv()

        def part(i, carry):
            held = [
                votes[r, j, pl.ds(pl.multiple_of(i * words, words), words)] for r in range(workers)
            ]
            directions = []
            for bit in range(32):
                count = sum(((h >> bit) & 1) for h in held)
                twice = 2 * count - workers
                directions.append(jnp.minimum(jnp.maximum(twice, -1), 1))
            direction = jnp.concatenate(directions, 0).astype(jnp.float32)
            at = pl.ds(pl.multiple_of(j * width + i * sub, sub), sub)
            upd_out[at, :] = (w_ref[at, :].astype(jnp.float32) - step_rate * direction).astype(
                jnp.bfloat16
            )
            return carry

        lax.fori_loop(0, width // sub, part, 0)

    def finish_grad(j):
        total[...] = term(j, z)
        for way in range(2):
            @pl.when(places[way] > 0)
            def _():
                any_hop(way, j, n - 1).wait_recv()
                came = sums[j, z] if way == 0 else last_sum[j]
                total[...] += came.astype(jnp.float32)

        grad_out[:, columns(j)] = (total[...] * mask_ref[...]).astype(jnp.bfloat16)

    def each(function, group):
        def one(half, carry):
            function(group * lanes + half)
            return carry

        lax.fori_loop(0, lanes, one, 0)

    groups = chunks // lanes
    loads[0].wait()
    each(send_own, 0)
    for load in loads[1:]:
        load.wait()

    def one_group(group, carry):
        for k in range(n - 1):
            each(lambda j: slot(j, k), group)
            if k == 0:
                @pl.when(group + 1 < groups)
                def _():
                    each(send_own, group + 1)

                @pl.when(group > 0)
                def _():
                    each(momentum_step, group - 1)

                @pl.when(group > 1)
                def _():
                    each(weight_step, group - 2)

                @pl.when(group > 0)
                def _():
                    each(finish_grad, group - 1)

        return carry

    lax.fori_loop(0, groups, one_group, 0)
    each(momentum_step, groups - 1)
    if groups > 1:
        each(weight_step, groups - 2)
    each(weight_step, groups - 1)
    each(finish_grad, groups - 1)

    def drain(j, carry):
        for way in range(2):
            @pl.when(places[way] < n - 1)
            def _():
                for k in range(n):
                    any_hop(way, j, k).wait_send()
        for step in range(1, workers):
            vote_copy(j, step, worker).wait_send()
        return carry

    lax.fori_loop(0, chunks, drain, 0)


def per_device(tokens_in, key_cot, row_mask, w_key, momentum):
    rows, features = tokens_in.shape
    head_cols = w_key.shape[1]
    n = lax.axis_size("tensor")
    workers = lax.axis_size("dp")
    sub = 256
    chunks = 10
    lanes = 2
    width = features // chunks
    bf16 = jnp.bfloat16
    vmem = pl.BlockSpec(memory_space=pltpu.VMEM)
    hbm = pl.BlockSpec(memory_space=pl.ANY)
    dma = pltpu.SemaphoreType.DMA
    input_grad, new_momentum, updated = pl.pallas_call(
        functools.partial(line_kernel, n, workers, chunks, lanes, sub),
        out_shape=(
            pltpu.VMEM((rows, features), bf16),
            pltpu.VMEM((features, head_cols), bf16),
            pltpu.VMEM((features, head_cols), bf16),
        ),
        in_specs=[hbm, hbm, vmem, hbm, hbm],
        out_specs=(vmem, vmem, vmem),
        scratch_shapes=[
            pltpu.VMEM((rows, features), bf16),
            pltpu.VMEM(key_cot.shape, bf16),
            pltpu.VMEM((features, head_cols), bf16),
            pltpu.VMEM((features, head_cols), bf16),
            pltpu.VMEM((chunks, n * rows, width), bf16),
            pltpu.VMEM((chunks, n, rows, width), bf16),
            pltpu.VMEM((chunks, rows, width), bf16),
            pltpu.VMEM((rows, width), jnp.float32),
            pltpu.VMEM((workers, chunks, width // 32, head_cols), jnp.int32),
            dma((2, chunks, n)),
            dma((2, chunks, n)),
            dma((workers, chunks)),
            dma((workers, chunks)),
            dma((4,)),
        ],
        compiler_params=pltpu.CompilerParams(
            collective_id=0, has_side_effects=True, vmem_limit_bytes=56 * 2**20
        ),
        cost_estimate=pl.CostEstimate(
            flops=4 * n * rows * features * head_cols,
            bytes_accessed=2 * (2 * rows * features + 4 * features * head_cols),
            transcendentals=0,
        ),
    )(tokens_in, key_cot, row_mask.astype(jnp.float32)[:, None], w_key, momentum[0])
    column_block = updated
    position = lax.axis_index("tensor")
    for depth_bit in range((n // 4).bit_length() - 1):
        partner = swapped(column_block, "tensor", depth_bit)
        lower_half = jnp.bitwise_and(jnp.right_shift(position, depth_bit), 1) == 0
        column_block = jnp.where(
            lower_half,
            jnp.concatenate([column_block, partner], 1),
            jnp.concatenate([partner, column_block], 1),
        )
    return (input_grad, new_momentum[None], column_block[None])


def solution(mesh):
    return jax.shard_map(
        per_device,
        mesh=mesh,
        in_specs=(
            P(("section", "dp", "tensor"), None),
            P(("section", "dp"), "tensor"),
            P(("section", "dp", "tensor")),
            P("section", "tensor"),
            P("dp", "section", "tensor"),
        ),
        out_specs=(
            P(("section", "dp", "tensor"), None),
            P("dp", "section", "tensor"),
            P("tensor", "section", None),
        ),
        check_vma=False,
    )
```

```python
import functools

import jax
import jax.numpy as jnp
from jax import lax
from jax.experimental import pallas as pl
from jax.experimental.pallas import tpu as pltpu
from jax.sharding import PartitionSpec as P

beta_slow = 0.99
beta_vote = 0.9
step_rate = 0.02
MESH = pl.DeviceIdType.MESH


def swapped(array, axis, stride):
    return lax.ppermute(array, axis, [(i, i ^ 1 << stride) for i in range(lax.axis_size(axis))])


def line_kernel(
    n, workers, chunks, lanes, sub,
    tok_in, cot_in, mask_in, w_in, mom_in,
    grad_out, mom_out, upd_out,
    tok_ref, cot_ref, w_ref, mom_ref, mask_ref,
    gathered, sums, last_sum, total, votes,
    send_sem, recv_sem, vote_send, vote_recv, in_sem,
):
    z = lax.axis_index("tensor")
    worker = lax.axis_index("dp")
    loads = [
        pltpu.make_async_copy(src, dst, in_sem.at[i])
        for i, (src, dst) in enumerate(
            ((tok_in, tok_ref), (cot_in, cot_ref), (w_in, w_ref), (mom_in, mom_ref))
        )
    ]
    for load in loads:
        load.start()
    rows = tok_ref.shape[0]
    width = tok_ref.shape[1] // chunks
    words = sub // 32

    barrier = pltpu.get_barrier_semaphore()

    @pl.when(z > 0)
    def _():
        pl.semaphore_signal(barrier, inc=1, device_id={"tensor": z - 1}, device_id_type=MESH)

    @pl.when(z < n - 1)
    def _():
        pl.semaphore_signal(barrier, inc=1, device_id={"tensor": z + 1}, device_id_type=MESH)

    for step in range(1, workers):
        pl.semaphore_signal(
            barrier, inc=1, device_id={"dp": lax.rem(worker + step, workers)}, device_id_type=MESH
        )

    places = (z, n - 1 - z)

    def named(way, index):
        return index if way == 0 else n - 1 - index

    def block(index):
        return pl.ds(pl.multiple_of(index * rows, rows), rows)

    def columns(j):
        return pl.ds(pl.multiple_of(j * width, width), width)

    def hop(way, j, k, src, dst):
        return pltpu.make_async_remote_copy(
            src_ref=src,
            dst_ref=dst,
            send_sem=send_sem.at[way, j, k],
            recv_sem=recv_sem.at[way, j, k],
            device_id={"tensor": z + 1 if way == 0 else z - 1},
            device_id_type=MESH,
        )

    def any_hop(way, j, k):
        return hop(way, j, k, last_sum.at[j], last_sum.at[j])

    def term(j, d):
        return lax.dot_general(
            cot_ref[block(d), :], w_ref[columns(j), :],
            (((1,), (1,)), ((), ())), preferred_element_type=jnp.float32,
        )

    def send_tokens(way, j, k, shard):
        piece = gathered.at[j, block(shard)]
        hop(way, j, k, piece, piece).start()

    def mask_own(j):
        gathered[j, block(z)] = (
            tok_ref[:, columns(j)].astype(jnp.float32) * mask_ref[...]
        ).astype(jnp.bfloat16)

    def send_own(j):
        for way in range(2):
            @pl.when(places[way] < n - 1)
            def _():
                send_tokens(way, j, 0, z)

    def slot(j, k):
        for way in range(2):
            place = places[way]

            @pl.when(place > 0)
            def _():
                any_hop(way, j, k).wait_recv()

            @pl.when(jnp.logical_and(k + 1 <= place, place < n - 1))
            def _():
                send_tokens(way, j, k + 1, named(way, place - 1 - k))

            @pl.when(k + 1 > place)
            def _():
                d = named(way, n + place - k - 1)
                total[...] = term(j, d)

                @pl.when(place > 0)
                def _():
                    total[...] += sums[j, d].astype(jnp.float32)

                sums[j, d] = total[...].astype(jnp.bfloat16)
                src = sums.at[j, d]
                dst = last_sum.at[j] if way == 1 and k + 1 == n - 1 else src
                hop(way, j, k + 1, src, dst).start()

    def vote_copy(j, step, source):
        piece = votes.at[source, j]
        return pltpu.make_async_remote_copy(
            src_ref=piece,
            dst_ref=piece,
            send_sem=vote_send.at[step, j],
            recv_sem=vote_recv.at[step, j],
            device_id={"dp": lax.rem(worker + step, workers)},
            device_id_type=MESH,
        )

    def momentum_step(j):
        def part(i, carry):
            at = pl.ds(pl.multiple_of(j * width + i * sub, sub), sub)
            key_grad = lax.dot_general(
                gathered[j, :, pl.ds(pl.multiple_of(i * sub, sub), sub)], cot_ref[...],
                (((0,), (0,)), ((), ())), preferred_element_type=jnp.float32,
            )
            prior = mom_ref[at, :].astype(jnp.float32)
            mom_out[at, :] = (beta_slow * prior + (1.0 - beta_slow) * key_grad).astype(jnp.bfloat16)
            interp = beta_vote * prior + (1.0 - beta_vote) * key_grad
            positive = (interp > 0).astype(jnp.int32)
            packed = positive[:words]
            for bit in range(1, 32):
                packed = packed | (positive[bit * words : (bit + 1) * words] << bit)
            votes[worker, j, pl.ds(pl.multiple_of(i * words, words), words)] = packed
            return carry

        lax.fori_loop(0, width // sub, part, 0)
        for step in range(1, workers):
            vote_copy(j, step, worker).start()

    def weight_step(j):
        for step in range(1, workers):
            vote_copy(j, step, worker).wait_recv()

        def part(i, carry):
            held = [
                votes[r, j, pl.ds(pl.multiple_of(i * words, words), words)] for r in range(workers)
            ]
            directions = []
            for bit in range(32):
                count = sum(((h >> bit) & 1) for h in held)
                twice = 2 * count - workers
                directions.append(jnp.minimum(jnp.maximum(twice, -1), 1))
            direction = jnp.concatenate(directions, 0).astype(jnp.float32)
            at = pl.ds(pl.multiple_of(j * width + i * sub, sub), sub)
            upd_out[at, :] = (w_ref[at, :].astype(jnp.float32) - step_rate * direction).astype(
                jnp.bfloat16
            )
            return carry

        lax.fori_loop(0, width // sub, part, 0)

    def finish_grad(j):
        total[...] = term(j, z)
        for way in range(2):
            @pl.when(places[way] > 0)
            def _():
                any_hop(way, j, n - 1).wait_recv()
                came = sums[j, z] if way == 0 else last_sum[j]
                total[...] += came.astype(jnp.float32)

        grad_out[:, columns(j)] = (total[...] * mask_ref[...]).astype(jnp.bfloat16)

    def each(function, group):
        def one(half, carry):
            function(group * lanes + half)
            return carry

        lax.fori_loop(0, lanes, one, 0)

    groups = chunks // lanes
    square = (rows, rows)
    diagonal = lax.broadcasted_iota(jnp.int32, square, 0) == lax.broadcasted_iota(
        jnp.int32, square, 1
    )
    spread = jnp.broadcast_to(mask_in[...].astype(jnp.float32), square)
    mask_ref[...] = jnp.sum(jnp.where(diagonal, spread, 0.0), axis=1, keepdims=True)
    loads[0].wait()
    each(mask_own, 0)

    @pl.when(jnp.logical_and(z > 0, z < n - 1))
    def _():
        pl.semaphore_wait(barrier, workers + 1)

    @pl.when(jnp.logical_or(z == 0, z == n - 1))
    def _():
        pl.semaphore_wait(barrier, workers)

    each(send_own, 0)
    for load in loads[1:]:
        load.wait()

    def one_group(group, carry):
        for k in range(n - 1):
            each(lambda j: slot(j, k), group)
            if k == 0:
                @pl.when(group + 1 < groups)
                def _():
                    each(mask_own, group + 1)
                    each(send_own, group + 1)

            @pl.when(group > 0)
            def _():
                if k == 0:
                    each(momentum_step, group - 1)
                if k == min(1, n - 2):
                    each(finish_grad, group - 1)
                if k == n - 2:
                    each(weight_step, group - 1)

        return carry

    lax.fori_loop(0, groups, one_group, 0)
    each(momentum_step, groups - 1)
    each(weight_step, groups - 1)
    each(finish_grad, groups - 1)

    def drain(j, carry):
        for way in range(2):
            @pl.when(places[way] < n - 1)
            def _():
                for k in range(n):
                    any_hop(way, j, k).wait_send()
        for step in range(1, workers):
            vote_copy(j, step, worker).wait_send()
        return carry

    lax.fori_loop(0, chunks, drain, 0)


def store_kernel(pieces, *refs):
    count = len(refs) // 2
    sem = refs[-1]
    copies = []
    for source, target in zip(refs[:count], refs[count : 2 * count]):
        step = source.shape[0] // pieces
        for piece in range(pieces):
            at = pl.ds(piece * step, step)
            copies.append(
                pltpu.make_async_copy(source.at[at], target.at[at], sem.at[len(copies)])
            )
    for copy in copies:
        copy.start()
    for copy in copies:
        copy.wait()


def stored(*arrays):
    pieces = 2
    return pl.pallas_call(
        functools.partial(store_kernel, pieces),
        out_shape=tuple(jax.ShapeDtypeStruct(a.shape, a.dtype) for a in arrays),
        in_specs=[pl.BlockSpec(memory_space=pltpu.VMEM)] * len(arrays),
        out_specs=tuple(pl.BlockSpec(memory_space=pl.ANY) for _ in arrays),
        scratch_shapes=[pltpu.SemaphoreType.DMA((pieces * len(arrays),))],
        compiler_params=pltpu.CompilerParams(vmem_limit_bytes=16 * 2**20),
    )(*arrays)


def per_device(tokens_in, key_cot, row_mask, w_key, momentum):
    rows, features = tokens_in.shape
    head_cols = w_key.shape[1]
    n = lax.axis_size("tensor")
    workers = lax.axis_size("dp")
    sub = 256
    chunks = 10
    lanes = 2
    width = features // chunks
    bf16 = jnp.bfloat16
    vmem = pl.BlockSpec(memory_space=pltpu.VMEM)
    hbm = pl.BlockSpec(memory_space=pl.ANY)
    dma = pltpu.SemaphoreType.DMA
    input_grad, new_momentum, updated = pl.pallas_call(
        functools.partial(line_kernel, n, workers, chunks, lanes, sub),
        out_shape=(
            pltpu.VMEM((rows, features), bf16),
            pltpu.VMEM((features, head_cols), bf16),
            pltpu.VMEM((features, head_cols), bf16),
        ),
        in_specs=[hbm, hbm, vmem, hbm, hbm],
        out_specs=(vmem, vmem, vmem),
        scratch_shapes=[
            pltpu.VMEM((rows, features), bf16),
            pltpu.VMEM(key_cot.shape, bf16),
            pltpu.VMEM((features, head_cols), bf16),
            pltpu.VMEM((features, head_cols), bf16),
            pltpu.VMEM((rows, 1), jnp.float32),
            pltpu.VMEM((chunks, n * rows, width), bf16),
            pltpu.VMEM((chunks, n, rows, width), bf16),
            pltpu.VMEM((chunks, rows, width), bf16),
            pltpu.VMEM((rows, width), jnp.float32),
            pltpu.VMEM((workers, chunks, width // 32, head_cols), jnp.int32),
            dma((2, chunks, n)),
            dma((2, chunks, n)),
            dma((workers, chunks)),
            dma((workers, chunks)),
            dma((4,)),
        ],
        compiler_params=pltpu.CompilerParams(
            collective_id=0, has_side_effects=True, vmem_limit_bytes=56 * 2**20
        ),
        cost_estimate=pl.CostEstimate(
            flops=4 * n * rows * features * head_cols,
            bytes_accessed=2 * (2 * rows * features + 4 * features * head_cols),
            transcendentals=0,
        ),
    )(tokens_in, key_cot, row_mask[None], w_key, momentum[0])
    input_grad, new_momentum, updated = stored(input_grad, new_momentum, updated)
    column_block = updated
    position = lax.axis_index("tensor")
    for depth_bit in range((n // 4).bit_length() - 1):
        partner = swapped(column_block, "tensor", depth_bit)
        lower_half = jnp.bitwise_and(jnp.right_shift(position, depth_bit), 1) == 0
        column_block = jnp.where(
            lower_half,
            jnp.concatenate([column_block, partner], 1),
            jnp.concatenate([partner, column_block], 1),
        )
    return (input_grad, new_momentum[None], column_block[None])


def solution(mesh):
    return jax.shard_map(
        per_device,
        mesh=mesh,
        in_specs=(
            P(("section", "dp", "tensor"), None),
            P(("section", "dp"), "tensor"),
            P(("section", "dp", "tensor")),
            P("section", "tensor"),
            P("dp", "section", "tensor"),
        ),
        out_specs=(
            P(("section", "dp", "tensor"), None),
            P("dp", "section", "tensor"),
            P("tensor", "section", None),
        ),
        check_vma=False,
    )
```

```python
import functools

import jax
import jax.numpy as jnp
from jax import lax
from jax.experimental import pallas as pl
from jax.experimental.pallas import tpu as pltpu
from jax.sharding import PartitionSpec as P

beta_slow = 0.99
beta_vote = 0.9
step_rate = 0.02
MESH = pl.DeviceIdType.MESH


def swapped(array, axis, stride):
    return lax.ppermute(array, axis, [(i, i ^ 1 << stride) for i in range(lax.axis_size(axis))])


def line_kernel(
    n, workers, chunks, lanes, ahead, sub,
    tok_in, cot_in, mask_in, w_in, mom_in,
    grad_out, mom_out, upd_out,
    tok_ref, cot_ref, w_ref, mom_ref, mask_ref,
    gathered, sums, last_sum, total, votes,
    send_sem, recv_sem, vote_send, vote_recv, in_sem,
):
    z = lax.axis_index("tensor")
    worker = lax.axis_index("dp")
    loads = [
        pltpu.make_async_copy(src, dst, in_sem.at[i])
        for i, (src, dst) in enumerate(
            ((tok_in, tok_ref), (cot_in, cot_ref), (w_in, w_ref), (mom_in, mom_ref))
        )
    ]
    for load in loads:
        load.start()
    rows = tok_ref.shape[0]
    width = tok_ref.shape[1] // chunks
    words = sub // 32

    barrier = pltpu.get_barrier_semaphore()

    @pl.when(z > 0)
    def _():
        pl.semaphore_signal(barrier, inc=1, device_id={"tensor": z - 1}, device_id_type=MESH)

    @pl.when(z < n - 1)
    def _():
        pl.semaphore_signal(barrier, inc=1, device_id={"tensor": z + 1}, device_id_type=MESH)

    for step in range(1, workers):
        pl.semaphore_signal(
            barrier, inc=1, device_id={"dp": lax.rem(worker + step, workers)}, device_id_type=MESH
        )

    places = (z, n - 1 - z)

    def named(way, index):
        return index if way == 0 else n - 1 - index

    def block(index):
        return pl.ds(pl.multiple_of(index * rows, rows), rows)

    def columns(j):
        return pl.ds(pl.multiple_of(j * width, width), width)

    def hop(way, j, k, src, dst):
        return pltpu.make_async_remote_copy(
            src_ref=src,
            dst_ref=dst,
            send_sem=send_sem.at[way, j, k],
            recv_sem=recv_sem.at[way, j, k],
            device_id={"tensor": z + 1 if way == 0 else z - 1},
            device_id_type=MESH,
        )

    def any_hop(way, j, k):
        return hop(way, j, k, last_sum.at[j], last_sum.at[j])

    def term(j, d):
        return lax.dot_general(
            cot_ref[block(d), :], w_ref[columns(j), :],
            (((1,), (1,)), ((), ())), preferred_element_type=jnp.float32,
        )

    def send_tokens(way, j, k, shard):
        piece = gathered.at[j, block(shard)]
        hop(way, j, k, piece, piece).start()

    def mask_own(j):
        gathered[j, block(z)] = (
            tok_ref[:, columns(j)].astype(jnp.float32) * mask_ref[...]
        ).astype(jnp.bfloat16)

    def send_own(j):
        for way in range(2):
            @pl.when(places[way] < n - 1)
            def _():
                send_tokens(way, j, 0, z)

    def slot(j, k):
        for way in range(2):
            place = places[way]

            @pl.when(place > 0)
            def _():
                any_hop(way, j, k).wait_recv()

            @pl.when(jnp.logical_and(k + 1 <= place, place < n - 1))
            def _():
                send_tokens(way, j, k + 1, named(way, place - 1 - k))

            @pl.when(k + 1 > place)
            def _():
                d = named(way, n + place - k - 1)
                total[...] = term(j, d)

                @pl.when(place > 0)
                def _():
                    total[...] += sums[j, d].astype(jnp.float32)

                sums[j, d] = total[...].astype(jnp.bfloat16)
                src = sums.at[j, d]
                dst = last_sum.at[j] if way == 1 and k + 1 == n - 1 else src
                hop(way, j, k + 1, src, dst).start()

    def vote_copy(j, step, source):
        piece = votes.at[source, j]
        return pltpu.make_async_remote_copy(
            src_ref=piece,
            dst_ref=piece,
            send_sem=vote_send.at[step, j],
            recv_sem=vote_recv.at[step, j],
            device_id={"dp": lax.rem(worker + step, workers)},
            device_id_type=MESH,
        )

    def momentum_step(j):
        def part(i, carry):
            at = pl.ds(pl.multiple_of(j * width + i * sub, sub), sub)
            key_grad = lax.dot_general(
                gathered[j, :, pl.ds(pl.multiple_of(i * sub, sub), sub)], cot_ref[...],
                (((0,), (0,)), ((), ())), preferred_element_type=jnp.float32,
            )
            prior = mom_ref[at, :].astype(jnp.float32)
            mom_out[at, :] = (beta_slow * prior + (1.0 - beta_slow) * key_grad).astype(jnp.bfloat16)
            interp = beta_vote * prior + (1.0 - beta_vote) * key_grad
            positive = (interp > 0).astype(jnp.int32)
            packed = positive[:words]
            for bit in range(1, 32):
                packed = packed | (positive[bit * words : (bit + 1) * words] << bit)
            votes[worker, j, pl.ds(pl.multiple_of(i * words, words), words)] = packed
            return carry

        lax.fori_loop(0, width // sub, part, 0)
        for step in range(1, workers):
            vote_copy(j, step, worker).start()

    def weight_step(j):
        for step in range(1, workers):
            vote_copy(j, step, worker).wait_recv()

        def part(i, carry):
            held = [
                votes[r, j, pl.ds(pl.multiple_of(i * words, words), words)] for r in range(workers)
            ]
            directions = []
            for bit in range(32):
                count = sum(((h >> bit) & 1) for h in held)
                twice = 2 * count - workers
                directions.append(jnp.minimum(jnp.maximum(twice, -1), 1))
            direction = jnp.concatenate(directions, 0).astype(jnp.float32)
            at = pl.ds(pl.multiple_of(j * width + i * sub, sub), sub)
            upd_out[at, :] = (w_ref[at, :].astype(jnp.float32) - step_rate * direction).astype(
                jnp.bfloat16
            )
            return carry

        lax.fori_loop(0, width // sub, part, 0)

    def finish_grad(j):
        total[...] = term(j, z)
        for way in range(2):
            @pl.when(places[way] > 0)
            def _():
                any_hop(way, j, n - 1).wait_recv()
                came = sums[j, z] if way == 0 else last_sum[j]
                total[...] += came.astype(jnp.float32)

        grad_out[:, columns(j)] = (total[...] * mask_ref[...]).astype(jnp.bfloat16)

    def each(function, group):
        def one(half, carry):
            function(group * lanes + half)
            return carry

        lax.fori_loop(0, lanes, one, 0)

    groups = chunks // lanes
    square = (rows, rows)
    diagonal = lax.broadcasted_iota(jnp.int32, square, 0) == lax.broadcasted_iota(
        jnp.int32, square, 1
    )
    spread = jnp.broadcast_to(mask_in[...].astype(jnp.float32), square)
    mask_ref[...] = jnp.sum(jnp.where(diagonal, spread, 0.0), axis=1, keepdims=True)
    loads[0].wait()
    for group in range(ahead):
        each(mask_own, group)

    @pl.when(jnp.logical_and(z > 0, z < n - 1))
    def _():
        pl.semaphore_wait(barrier, workers + 1)

    @pl.when(jnp.logical_or(z == 0, z == n - 1))
    def _():
        pl.semaphore_wait(barrier, workers)

    for group in range(ahead):
        each(send_own, group)
    for load in loads[1:]:
        load.wait()

    def one_group(group, carry):
        for k in range(n - 1):
            each(lambda j: slot(j, k), group)
            if k == 0:
                @pl.when(group + ahead < groups)
                def _():
                    each(mask_own, group + ahead)
                    each(send_own, group + ahead)

            @pl.when(group > 0)
            def _():
                if k == 0:
                    each(momentum_step, group - 1)
                if k == min(1, n - 2):
                    each(finish_grad, group - 1)
                if k == n - 2:
                    each(weight_step, group - 1)

        return carry

    lax.fori_loop(0, groups, one_group, 0)
    each(momentum_step, groups - 1)
    each(weight_step, groups - 1)
    each(finish_grad, groups - 1)

    def drain(j, carry):
        for way in range(2):
            @pl.when(places[way] < n - 1)
            def _():
                for k in range(n):
                    any_hop(way, j, k).wait_send()
        for step in range(1, workers):
            vote_copy(j, step, worker).wait_send()
        return carry

    lax.fori_loop(0, chunks, drain, 0)


def store_kernel(pieces, *refs):
    count = len(refs) // 2
    sem = refs[-1]
    copies = []
    for source, target in zip(refs[:count], refs[count : 2 * count]):
        step = source.shape[0] // pieces
        for piece in range(pieces):
            at = pl.ds(piece * step, step)
            copies.append(
                pltpu.make_async_copy(source.at[at], target.at[at], sem.at[len(copies)])
            )
    for copy in copies:
        copy.start()
    for copy in copies:
        copy.wait()


def stored(*arrays):
    pieces = 2
    return pl.pallas_call(
        functools.partial(store_kernel, pieces),
        out_shape=tuple(jax.ShapeDtypeStruct(a.shape, a.dtype) for a in arrays),
        in_specs=[pl.BlockSpec(memory_space=pltpu.VMEM)] * len(arrays),
        out_specs=tuple(pl.BlockSpec(memory_space=pl.ANY) for _ in arrays),
        scratch_shapes=[pltpu.SemaphoreType.DMA((pieces * len(arrays),))],
        compiler_params=pltpu.CompilerParams(vmem_limit_bytes=16 * 2**20),
    )(*arrays)


def per_device(tokens_in, key_cot, row_mask, w_key, momentum):
    rows, features = tokens_in.shape
    head_cols = w_key.shape[1]
    n = lax.axis_size("tensor")
    workers = lax.axis_size("dp")
    sub = 256
    chunks = 20
    ahead = 2
    lanes = 2
    width = features // chunks
    bf16 = jnp.bfloat16
    vmem = pl.BlockSpec(memory_space=pltpu.VMEM)
    hbm = pl.BlockSpec(memory_space=pl.ANY)
    dma = pltpu.SemaphoreType.DMA
    input_grad, new_momentum, updated = pl.pallas_call(
        functools.partial(line_kernel, n, workers, chunks, lanes, ahead, sub),
        out_shape=(
            pltpu.VMEM((rows, features), bf16),
            pltpu.VMEM((features, head_cols), bf16),
            pltpu.VMEM((features, head_cols), bf16),
        ),
        in_specs=[hbm, hbm, vmem, hbm, hbm],
        out_specs=(vmem, vmem, vmem),
        scratch_shapes=[
            pltpu.VMEM((rows, features), bf16),
            pltpu.VMEM(key_cot.shape, bf16),
            pltpu.VMEM((features, head_cols), bf16),
            pltpu.VMEM((features, head_cols), bf16),
            pltpu.VMEM((rows, 1), jnp.float32),
            pltpu.VMEM((chunks, n * rows, width), bf16),
            pltpu.VMEM((chunks, n, rows, width), bf16),
            pltpu.VMEM((chunks, rows, width), bf16),
            pltpu.VMEM((rows, width), jnp.float32),
            pltpu.VMEM((workers, chunks, width // 32, head_cols), jnp.int32),
            dma((2, chunks, n)),
            dma((2, chunks, n)),
            dma((workers, chunks)),
            dma((workers, chunks)),
            dma((4,)),
        ],
        compiler_params=pltpu.CompilerParams(
            collective_id=0, has_side_effects=True, vmem_limit_bytes=56 * 2**20
        ),
        cost_estimate=pl.CostEstimate(
            flops=4 * n * rows * features * head_cols,
            bytes_accessed=2 * (2 * rows * features + 4 * features * head_cols),
            transcendentals=0,
        ),
    )(tokens_in, key_cot, row_mask[None], w_key, momentum[0])
    input_grad, new_momentum, updated = stored(input_grad, new_momentum, updated)
    column_block = updated
    position = lax.axis_index("tensor")
    for depth_bit in range((n // 4).bit_length() - 1):
        partner = swapped(column_block, "tensor", depth_bit)
        lower_half = jnp.bitwise_and(jnp.right_shift(position, depth_bit), 1) == 0
        column_block = jnp.where(
            lower_half,
            jnp.concatenate([column_block, partner], 1),
            jnp.concatenate([partner, column_block], 1),
        )
    return (input_grad, new_momentum[None], column_block[None])


def solution(mesh):
    return jax.shard_map(
        per_device,
        mesh=mesh,
        in_specs=(
            P(("section", "dp", "tensor"), None),
            P(("section", "dp"), "tensor"),
            P(("section", "dp", "tensor")),
            P("section", "tensor"),
            P("dp", "section", "tensor"),
        ),
        out_specs=(
            P(("section", "dp", "tensor"), None),
            P("dp", "section", "tensor"),
            P("tensor", "section", None),
        ),
        check_vma=False,
    )
```

```python
import functools

import jax
import jax.numpy as jnp
from jax import lax
from jax.experimental import pallas as pl
from jax.experimental.pallas import tpu as pltpu
from jax.sharding import PartitionSpec as P

beta_slow = 0.99
beta_vote = 0.9
step_rate = 0.02
MESH = pl.DeviceIdType.MESH


def swapped(array, axis, stride):
    return lax.ppermute(array, axis, [(i, i ^ 1 << stride) for i in range(lax.axis_size(axis))])


def line_kernel(
    n, workers, chunks, lanes, ahead, sub,
    tok_in, cot_in, mask_in, w_in, mom_in,
    grad_out, mom_out, upd_out,
    tok_ref, cot_ref, w_ref, mom_ref, mask_ref,
    gathered, sums, last_sum, total, votes,
    send_sem, recv_sem, vote_send, vote_recv, in_sem,
):
    z = lax.axis_index("tensor")
    worker = lax.axis_index("dp")
    loads = [
        pltpu.make_async_copy(src, dst, in_sem.at[i])
        for i, (src, dst) in enumerate(
            ((tok_in, tok_ref), (cot_in, cot_ref), (w_in, w_ref), (mom_in, mom_ref))
        )
    ]
    for load in loads:
        load.start()
    rows = tok_ref.shape[0]
    width = tok_ref.shape[1] // chunks
    words = sub // 32

    barrier = pltpu.get_barrier_semaphore()

    @pl.when(z > 0)
    def _():
        pl.semaphore_signal(barrier, inc=1, device_id={"tensor": z - 1}, device_id_type=MESH)

    @pl.when(z < n - 1)
    def _():
        pl.semaphore_signal(barrier, inc=1, device_id={"tensor": z + 1}, device_id_type=MESH)

    for step in range(1, workers):
        pl.semaphore_signal(
            barrier, inc=1, device_id={"dp": lax.rem(worker + step, workers)}, device_id_type=MESH
        )

    places = (z, n - 1 - z)

    def named(way, index):
        return index if way == 0 else n - 1 - index

    def block(index):
        return pl.ds(pl.multiple_of(index * rows, rows), rows)

    def columns(j):
        return pl.ds(pl.multiple_of(j * width, width), width)

    def hop(way, j, k, src, dst):
        return pltpu.make_async_remote_copy(
            src_ref=src,
            dst_ref=dst,
            send_sem=send_sem.at[way, j, k],
            recv_sem=recv_sem.at[way, j, k],
            device_id={"tensor": z + 1 if way == 0 else z - 1},
            device_id_type=MESH,
        )

    def any_hop(way, j, k):
        return hop(way, j, k, last_sum.at[j], last_sum.at[j])

    def term(j, d):
        return lax.dot_general(
            cot_ref[block(d), :], w_ref[columns(j), :],
            (((1,), (1,)), ((), ())), preferred_element_type=jnp.float32,
        )

    def send_tokens(way, j, k, shard):
        piece = gathered.at[j, block(shard)]
        hop(way, j, k, piece, piece).start()

    def mask_own(j):
        gathered[j, block(z)] = (
            tok_ref[:, columns(j)].astype(jnp.float32) * mask_ref[...]
        ).astype(jnp.bfloat16)

    def send_own(j):
        for way in range(2):
            @pl.when(places[way] < n - 1)
            def _():
                send_tokens(way, j, 0, z)

    def slot(j, k):
        for way in range(2):
            place = places[way]

            @pl.when(place > 0)
            def _():
                any_hop(way, j, k).wait_recv()

            @pl.when(jnp.logical_and(k + 1 <= place, place < n - 1))
            def _():
                send_tokens(way, j, k + 1, named(way, place - 1 - k))

            @pl.when(k + 1 > place)
            def _():
                d = named(way, n + place - k - 1)
                total[...] = term(j, d)

                @pl.when(place > 0)
                def _():
                    total[...] += sums[j, d].astype(jnp.float32)

                sums[j, d] = total[...].astype(jnp.bfloat16)
                src = sums.at[j, d]
                dst = last_sum.at[j] if way == 1 and k + 1 == n - 1 else src
                hop(way, j, k + 1, src, dst).start()

    def vote_copy(j, step, source):
        piece = votes.at[source, j]
        return pltpu.make_async_remote_copy(
            src_ref=piece,
            dst_ref=piece,
            send_sem=vote_send.at[step, j],
            recv_sem=vote_recv.at[step, j],
            device_id={"dp": lax.rem(worker + step, workers)},
            device_id_type=MESH,
        )

    def momentum_step(j):
        def part(i, carry):
            at = pl.ds(pl.multiple_of(j * width + i * sub, sub), sub)
            key_grad = lax.dot_general(
                gathered[j, :, pl.ds(pl.multiple_of(i * sub, sub), sub)], cot_ref[...],
                (((0,), (0,)), ((), ())), preferred_element_type=jnp.float32,
            )
            prior = mom_ref[at, :].astype(jnp.float32)
            mom_out[at, :] = (beta_slow * prior + (1.0 - beta_slow) * key_grad).astype(jnp.bfloat16)
            interp = beta_vote * prior + (1.0 - beta_vote) * key_grad
            positive = (interp > 0).astype(jnp.int32)
            packed = positive[:words]
            for bit in range(1, 32):
                packed = packed | (positive[bit * words : (bit + 1) * words] << bit)
            votes[worker, j, pl.ds(pl.multiple_of(i * words, words), words)] = packed
            return carry

        lax.fori_loop(0, width // sub, part, 0)
        for step in range(1, workers):
            vote_copy(j, step, worker).start()

    def weight_step(j):
        for step in range(1, workers):
            vote_copy(j, step, worker).wait_recv()

        def part(i, carry):
            held = [
                votes[r, j, pl.ds(pl.multiple_of(i * words, words), words)] for r in range(workers)
            ]
            directions = []
            for bit in range(32):
                count = sum(((h >> bit) & 1) for h in held)
                twice = 2 * count - workers
                directions.append(jnp.minimum(jnp.maximum(twice, -1), 1))
            direction = jnp.concatenate(directions, 0).astype(jnp.float32)
            at = pl.ds(pl.multiple_of(j * width + i * sub, sub), sub)
            upd_out[at, :] = (w_ref[at, :].astype(jnp.float32) - step_rate * direction).astype(
                jnp.bfloat16
            )
            return carry

        lax.fori_loop(0, width // sub, part, 0)

    def finish_grad(j):
        total[...] = term(j, z)
        for way in range(2):
            @pl.when(places[way] > 0)
            def _():
                any_hop(way, j, n - 1).wait_recv()
                came = sums[j, z] if way == 0 else last_sum[j]
                total[...] += came.astype(jnp.float32)

        grad_out[:, columns(j)] = (total[...] * mask_ref[...]).astype(jnp.bfloat16)

    def each(function, group):
        def one(half, carry):
            function(group * lanes + half)
            return carry

        lax.fori_loop(0, lanes, one, 0)

    groups = chunks // lanes
    square = (rows, rows)
    diagonal = lax.broadcasted_iota(jnp.int32, square, 0) == lax.broadcasted_iota(
        jnp.int32, square, 1
    )
    spread = jnp.broadcast_to(mask_in[...].astype(jnp.float32), square)
    mask_ref[...] = jnp.sum(jnp.where(diagonal, spread, 0.0), axis=1, keepdims=True)
    loads[0].wait()
    for group in range(ahead):
        each(mask_own, group)

    @pl.when(jnp.logical_and(z > 0, z < n - 1))
    def _():
        pl.semaphore_wait(barrier, workers + 1)

    @pl.when(jnp.logical_or(z == 0, z == n - 1))
    def _():
        pl.semaphore_wait(barrier, workers)

    for group in range(ahead):
        each(send_own, group)
    for load in loads[1:]:
        load.wait()

    def one_group(group, carry):
        for k in range(n - 1):
            each(lambda j: slot(j, k), group)
            if k == 0:
                @pl.when(group + ahead < groups)
                def _():
                    each(mask_own, group + ahead)
                    each(send_own, group + ahead)

            @pl.when(group > 0)
            def _():
                if k == 0:
                    each(momentum_step, group - 1)
                if k == min(1, n - 2):
                    each(finish_grad, group - 1)
                if k == n - 2:
                    each(weight_step, group - 1)

        return carry

    lax.fori_loop(0, groups, one_group, 0)
    each(momentum_step, groups - 1)
    each(weight_step, groups - 1)
    each(finish_grad, groups - 1)

    def drain(j, carry):
        for way in range(2):
            @pl.when(places[way] < n - 1)
            def _():
                for k in range(n):
                    any_hop(way, j, k).wait_send()
        for step in range(1, workers):
            vote_copy(j, step, worker).wait_send()
        return carry

    lax.fori_loop(0, chunks, drain, 0)


def store_kernel(pieces, *refs):
    count = len(refs) // 2
    sem = refs[-1]
    copies = []
    for source, target in zip(refs[:count], refs[count : 2 * count]):
        step = source.shape[0] // pieces
        for piece in range(pieces):
            at = pl.ds(piece * step, step)
            copies.append(
                pltpu.make_async_copy(source.at[at], target.at[at], sem.at[len(copies)])
            )
    for copy in copies:
        copy.start()
    for copy in copies:
        copy.wait()


def stored(*arrays):
    pieces = 2
    return pl.pallas_call(
        functools.partial(store_kernel, pieces),
        out_shape=tuple(jax.ShapeDtypeStruct(a.shape, a.dtype) for a in arrays),
        in_specs=[pl.BlockSpec(memory_space=pltpu.VMEM)] * len(arrays),
        out_specs=tuple(pl.BlockSpec(memory_space=pl.ANY) for _ in arrays),
        scratch_shapes=[pltpu.SemaphoreType.DMA((pieces * len(arrays),))],
        compiler_params=pltpu.CompilerParams(vmem_limit_bytes=16 * 2**20),
    )(*arrays)


def per_device(tokens_in, key_cot, row_mask, w_key, momentum):
    rows, features = tokens_in.shape
    head_cols = w_key.shape[1]
    n = lax.axis_size("tensor")
    workers = lax.axis_size("dp")
    sub = 256
    chunks = 10
    ahead = 2
    lanes = 2
    width = features // chunks
    bf16 = jnp.bfloat16
    vmem = pl.BlockSpec(memory_space=pltpu.VMEM)
    hbm = pl.BlockSpec(memory_space=pl.ANY)
    dma = pltpu.SemaphoreType.DMA
    input_grad, new_momentum, updated = pl.pallas_call(
        functools.partial(line_kernel, n, workers, chunks, lanes, ahead, sub),
        out_shape=(
            pltpu.VMEM((rows, features), bf16),
            pltpu.VMEM((features, head_cols), bf16),
            pltpu.VMEM((features, head_cols), bf16),
        ),
        in_specs=[hbm, hbm, vmem, hbm, hbm],
        out_specs=(vmem, vmem, vmem),
        scratch_shapes=[
            pltpu.VMEM((rows, features), bf16),
            pltpu.VMEM(key_cot.shape, bf16),
            pltpu.VMEM((features, head_cols), bf16),
            pltpu.VMEM((features, head_cols), bf16),
            pltpu.VMEM((rows, 1), jnp.float32),
            pltpu.VMEM((chunks, n * rows, width), bf16),
            pltpu.VMEM((chunks, n, rows, width), bf16),
            pltpu.VMEM((chunks, rows, width), bf16),
            pltpu.VMEM((rows, width), jnp.float32),
            pltpu.VMEM((workers, chunks, width // 32, head_cols), jnp.int32),
            dma((2, chunks, n)),
            dma((2, chunks, n)),
            dma((workers, chunks)),
            dma((workers, chunks)),
            dma((4,)),
        ],
        compiler_params=pltpu.CompilerParams(
            collective_id=0, has_side_effects=True, vmem_limit_bytes=56 * 2**20
        ),
        cost_estimate=pl.CostEstimate(
            flops=4 * n * rows * features * head_cols,
            bytes_accessed=2 * (2 * rows * features + 4 * features * head_cols),
            transcendentals=0,
        ),
    )(tokens_in, key_cot, row_mask[None], w_key, momentum[0])
    input_grad, new_momentum, updated = stored(input_grad, new_momentum, updated)
    column_block = updated
    position = lax.axis_index("tensor")
    for depth_bit in range((n // 4).bit_length() - 1):
        partner = swapped(column_block, "tensor", depth_bit)
        lower_half = jnp.bitwise_and(jnp.right_shift(position, depth_bit), 1) == 0
        column_block = jnp.where(
            lower_half,
            jnp.concatenate([column_block, partner], 1),
            jnp.concatenate([partner, column_block], 1),
        )
    return (input_grad, new_momentum[None], column_block[None])


def solution(mesh):
    return jax.shard_map(
        per_device,
        mesh=mesh,
        in_specs=(
            P(("section", "dp", "tensor"), None),
            P(("section", "dp"), "tensor"),
            P(("section", "dp", "tensor")),
            P("section", "tensor"),
            P("dp", "section", "tensor"),
        ),
        out_specs=(
            P(("section", "dp", "tensor"), None),
            P("dp", "section", "tensor"),
            P("tensor", "section", None),
        ),
        check_vma=False,
    )
```

```python
import functools

import jax
import jax.numpy as jnp
from jax import lax
from jax.experimental import pallas as pl
from jax.experimental.pallas import tpu as pltpu
from jax.sharding import PartitionSpec as P

beta_slow = 0.99
beta_vote = 0.9
step_rate = 0.02
MESH = pl.DeviceIdType.MESH


def swapped(array, axis, stride):
    return lax.ppermute(array, axis, [(i, i ^ 1 << stride) for i in range(lax.axis_size(axis))])


def line_kernel(
    n, workers, chunks, lanes, sub,
    tok_in, cot_in, mask_in, w_in, mom_in,
    grad_out, mom_out, upd_out,
    tok_ref, cot_ref, w_ref, mom_ref, mask_ref,
    gathered, sums, last_sum, total, votes,
    send_sem, recv_sem, vote_send, vote_recv, in_sem,
):
    z = lax.axis_index("tensor")
    worker = lax.axis_index("dp")
    first = pl.ds(0, tok_ref.shape[1] * lanes // chunks)
    rest = pl.ds(first.size, tok_ref.shape[1] - first.size)
    loads = [
        pltpu.make_async_copy(src, dst, in_sem.at[i])
        for i, (src, dst) in enumerate(
            (
                (tok_in.at[:, first], tok_ref.at[:, first]),
                (cot_in, cot_ref),
                (w_in, w_ref),
                (tok_in.at[:, rest], tok_ref.at[:, rest]),
                (mom_in, mom_ref),
            )
        )
    ]
    loads[0].start()
    rows = tok_ref.shape[0]
    width = tok_ref.shape[1] // chunks
    words = sub // 32

    barrier = pltpu.get_barrier_semaphore()

    @pl.when(z > 0)
    def _():
        pl.semaphore_signal(barrier, inc=1, device_id={"tensor": z - 1}, device_id_type=MESH)

    @pl.when(z < n - 1)
    def _():
        pl.semaphore_signal(barrier, inc=1, device_id={"tensor": z + 1}, device_id_type=MESH)

    for step in range(1, workers):
        pl.semaphore_signal(
            barrier, inc=1, device_id={"dp": lax.rem(worker + step, workers)}, device_id_type=MESH
        )

    places = (z, n - 1 - z)

    def named(way, index):
        return index if way == 0 else n - 1 - index

    def block(index):
        return pl.ds(pl.multiple_of(index * rows, rows), rows)

    def columns(j):
        return pl.ds(pl.multiple_of(j * width, width), width)

    def hop(way, j, k, src, dst):
        return pltpu.make_async_remote_copy(
            src_ref=src,
            dst_ref=dst,
            send_sem=send_sem.at[way, j, k],
            recv_sem=recv_sem.at[way, j, k],
            device_id={"tensor": z + 1 if way == 0 else z - 1},
            device_id_type=MESH,
        )

    def any_hop(way, j, k):
        return hop(way, j, k, last_sum.at[j], last_sum.at[j])

    def term(j, d):
        return lax.dot_general(
            cot_ref[block(d), :], w_ref[columns(j), :],
            (((1,), (1,)), ((), ())), preferred_element_type=jnp.float32,
        )

    def send_tokens(way, j, k, shard):
        piece = gathered.at[j, block(shard)]
        hop(way, j, k, piece, piece).start()

    def mask_own(j):
        gathered[j, block(z)] = (
            tok_ref[:, columns(j)].astype(jnp.float32) * mask_ref[...]
        ).astype(jnp.bfloat16)

    def send_own(j):
        for way in range(2):
            @pl.when(places[way] < n - 1)
            def _():
                send_tokens(way, j, 0, z)

    def slot(j, k):
        for way in range(2):
            place = places[way]

            @pl.when(place > 0)
            def _():
                any_hop(way, j, k).wait_recv()

            @pl.when(jnp.logical_and(k + 1 <= place, place < n - 1))
            def _():
                send_tokens(way, j, k + 1, named(way, place - 1 - k))

            @pl.when(k + 1 > place)
            def _():
                d = named(way, n + place - k - 1)
                total[...] = term(j, d)

                @pl.when(place > 0)
                def _():
                    total[...] += sums[j, d].astype(jnp.float32)

                sums[j, d] = total[...].astype(jnp.bfloat16)
                src = sums.at[j, d]
                dst = last_sum.at[j] if way == 1 and k + 1 == n - 1 else src
                hop(way, j, k + 1, src, dst).start()

    def vote_copy(j, step, source):
        piece = votes.at[source, j]
        return pltpu.make_async_remote_copy(
            src_ref=piece,
            dst_ref=piece,
            send_sem=vote_send.at[step, j],
            recv_sem=vote_recv.at[step, j],
            device_id={"dp": lax.rem(worker + step, workers)},
            device_id_type=MESH,
        )

    def momentum_step(j):
        def part(i, carry):
            at = pl.ds(pl.multiple_of(j * width + i * sub, sub), sub)
            key_grad = lax.dot_general(
                gathered[j, :, pl.ds(pl.multiple_of(i * sub, sub), sub)], cot_ref[...],
                (((0,), (0,)), ((), ())), preferred_element_type=jnp.float32,
            )
            prior = mom_ref[at, :].astype(jnp.float32)
            mom_out[at, :] = (beta_slow * prior + (1.0 - beta_slow) * key_grad).astype(jnp.bfloat16)
            interp = beta_vote * prior + (1.0 - beta_vote) * key_grad
            positive = (interp > 0).astype(jnp.int32)
            packed = positive[:words]
            for bit in range(1, 32):
                packed = packed | (positive[bit * words : (bit + 1) * words] << bit)
            votes[worker, j, pl.ds(pl.multiple_of(i * words, words), words)] = packed
            return carry

        lax.fori_loop(0, width // sub, part, 0)
        for step in range(1, workers):
            vote_copy(j, step, worker).start()

    def weight_step(j):
        for step in range(1, workers):
            vote_copy(j, step, worker).wait_recv()

        def part(i, carry):
            held = [
                votes[r, j, pl.ds(pl.multiple_of(i * words, words), words)] for r in range(workers)
            ]
            directions = []
            for bit in range(32):
                count = sum(((h >> bit) & 1) for h in held)
                twice = 2 * count - workers
                directions.append(jnp.minimum(jnp.maximum(twice, -1), 1))
            direction = jnp.concatenate(directions, 0).astype(jnp.float32)
            at = pl.ds(pl.multiple_of(j * width + i * sub, sub), sub)
            upd_out[at, :] = (w_ref[at, :].astype(jnp.float32) - step_rate * direction).astype(
                jnp.bfloat16
            )
            return carry

        lax.fori_loop(0, width // sub, part, 0)

    def finish_grad(j):
        total[...] = term(j, z)
        for way in range(2):
            @pl.when(places[way] > 0)
            def _():
                any_hop(way, j, n - 1).wait_recv()
                came = sums[j, z] if way == 0 else last_sum[j]
                total[...] += came.astype(jnp.float32)

        grad_out[:, columns(j)] = (total[...] * mask_ref[...]).astype(jnp.bfloat16)

    def each(function, group):
        def one(half, carry):
            function(group * lanes + half)
            return carry

        lax.fori_loop(0, lanes, one, 0)

    groups = chunks // lanes
    square = (rows, rows)
    diagonal = lax.broadcasted_iota(jnp.int32, square, 0) == lax.broadcasted_iota(
        jnp.int32, square, 1
    )
    spread = jnp.broadcast_to(mask_in[...].astype(jnp.float32), square)
    mask_ref[...] = jnp.sum(jnp.where(diagonal, spread, 0.0), axis=1, keepdims=True)
    loads[0].wait()
    for load in loads[1:]:
        load.start()
    each(mask_own, 0)

    @pl.when(jnp.logical_and(z > 0, z < n - 1))
    def _():
        pl.semaphore_wait(barrier, workers + 1)

    @pl.when(jnp.logical_or(z == 0, z == n - 1))
    def _():
        pl.semaphore_wait(barrier, workers)

    each(send_own, 0)
    for load in loads[1:]:
        load.wait()

    def one_group(group, carry):
        for k in range(n - 1):
            each(lambda j: slot(j, k), group)
            if k == 0:
                @pl.when(group + 1 < groups)
                def _():
                    each(mask_own, group + 1)
                    each(send_own, group + 1)

            @pl.when(group > 0)
            def _():
                if k == 0:
                    each(momentum_step, group - 1)
                if k == min(1, n - 2):
                    each(finish_grad, group - 1)
                    each(weight_step, group - 1)

        return carry

    lax.fori_loop(0, groups, one_group, 0)
    each(momentum_step, groups - 1)
    each(finish_grad, groups - 1)
    each(weight_step, groups - 1)

    def drain(j, carry):
        for way in range(2):
            @pl.when(places[way] < n - 1)
            def _():
                for k in range(n):
                    any_hop(way, j, k).wait_send()
        for step in range(1, workers):
            vote_copy(j, step, worker).wait_send()
        return carry

    lax.fori_loop(0, chunks, drain, 0)


def store_kernel(pieces, *refs):
    count = len(refs) // 2
    sem = refs[-1]
    copies = []
    for source, target in zip(refs[:count], refs[count : 2 * count]):
        step = source.shape[0] // pieces
        for piece in range(pieces):
            at = pl.ds(piece * step, step)
            copies.append(
                pltpu.make_async_copy(source.at[at], target.at[at], sem.at[len(copies)])
            )
    for copy in copies:
        copy.start()
    for copy in copies:
        copy.wait()


def stored(*arrays):
    pieces = 2
    return pl.pallas_call(
        functools.partial(store_kernel, pieces),
        out_shape=tuple(jax.ShapeDtypeStruct(a.shape, a.dtype) for a in arrays),
        in_specs=[pl.BlockSpec(memory_space=pltpu.VMEM)] * len(arrays),
        out_specs=tuple(pl.BlockSpec(memory_space=pl.ANY) for _ in arrays),
        scratch_shapes=[pltpu.SemaphoreType.DMA((pieces * len(arrays),))],
        compiler_params=pltpu.CompilerParams(vmem_limit_bytes=16 * 2**20),
    )(*arrays)


def per_device(tokens_in, key_cot, row_mask, w_key, momentum):
    rows, features = tokens_in.shape
    head_cols = w_key.shape[1]
    n = lax.axis_size("tensor")
    workers = lax.axis_size("dp")
    sub = 256
    chunks = 10
    lanes = 2
    width = features // chunks
    bf16 = jnp.bfloat16
    vmem = pl.BlockSpec(memory_space=pltpu.VMEM)
    hbm = pl.BlockSpec(memory_space=pl.ANY)
    dma = pltpu.SemaphoreType.DMA
    input_grad, new_momentum, updated = pl.pallas_call(
        functools.partial(line_kernel, n, workers, chunks, lanes, sub),
        out_shape=(
            pltpu.VMEM((rows, features), bf16),
            pltpu.VMEM((features, head_cols), bf16),
            pltpu.VMEM((features, head_cols), bf16),
        ),
        in_specs=[hbm, hbm, vmem, hbm, hbm],
        out_specs=(vmem, vmem, vmem),
        scratch_shapes=[
            pltpu.VMEM((rows, features), bf16),
            pltpu.VMEM(key_cot.shape, bf16),
            pltpu.VMEM((features, head_cols), bf16),
            pltpu.VMEM((features, head_cols), bf16),
            pltpu.VMEM((rows, 1), jnp.float32),
            pltpu.VMEM((chunks, n * rows, width), bf16),
            pltpu.VMEM((chunks, n, rows, width), bf16),
            pltpu.VMEM((chunks, rows, width), bf16),
            pltpu.VMEM((rows, width), jnp.float32),
            pltpu.VMEM((workers, chunks, width // 32, head_cols), jnp.int32),
            dma((2, chunks, n)),
            dma((2, chunks, n)),
            dma((workers, chunks)),
            dma((workers, chunks)),
            dma((5,)),
        ],
        compiler_params=pltpu.CompilerParams(
            collective_id=0, has_side_effects=True, vmem_limit_bytes=56 * 2**20
        ),
        cost_estimate=pl.CostEstimate(
            flops=4 * n * rows * features * head_cols,
            bytes_accessed=2 * (2 * rows * features + 4 * features * head_cols),
            transcendentals=0,
        ),
    )(tokens_in, key_cot, row_mask[None], w_key, momentum[0])
    input_grad, new_momentum, updated = stored(input_grad, new_momentum, updated)
    column_block = updated
    position = lax.axis_index("tensor")
    for depth_bit in range((n // 4).bit_length() - 1):
        partner = swapped(column_block, "tensor", depth_bit)
        lower_half = jnp.bitwise_and(jnp.right_shift(position, depth_bit), 1) == 0
        column_block = jnp.where(
            lower_half,
            jnp.concatenate([column_block, partner], 1),
            jnp.concatenate([partner, column_block], 1),
        )
    return (input_grad, new_momentum[None], column_block[None])


def solution(mesh):
    return jax.shard_map(
        per_device,
        mesh=mesh,
        in_specs=(
            P(("section", "dp", "tensor"), None),
            P(("section", "dp"), "tensor"),
            P(("section", "dp", "tensor")),
            P("section", "tensor"),
            P("dp", "section", "tensor"),
        ),
        out_specs=(
            P(("section", "dp", "tensor"), None),
            P("dp", "section", "tensor"),
            P("tensor", "section", None),
        ),
        check_vma=False,
    )
```

```python
import functools

import jax
import jax.numpy as jnp
from jax import lax
from jax.experimental import pallas as pl
from jax.experimental.pallas import tpu as pltpu
from jax.sharding import PartitionSpec as P

beta_slow = 0.99
beta_vote = 0.9
step_rate = 0.02
MESH = pl.DeviceIdType.MESH


def swapped(array, axis, stride):
    return lax.ppermute(array, axis, [(i, i ^ 1 << stride) for i in range(lax.axis_size(axis))])


def line_kernel(
    n, workers, chunks, lanes, sub,
    tok_in, cot_in, mask_in, w_in, mom_in,
    grad_out, mom_out, upd_out,
    tok_ref, cot_ref, w_ref, mom_ref, mask_ref,
    gathered, sums, last_sum, total, votes,
    send_sem, recv_sem, vote_send, vote_recv, in_sem,
):
    z = lax.axis_index("tensor")
    worker = lax.axis_index("dp")
    loads = [
        pltpu.make_async_copy(src, dst, in_sem.at[i])
        for i, (src, dst) in enumerate(
            ((tok_in, tok_ref), (cot_in, cot_ref), (w_in, w_ref), (mom_in, mom_ref))
        )
    ]
    for load in loads:
        load.start()
    rows = tok_ref.shape[0]
    width = tok_ref.shape[1] // chunks
    words = sub // 32

    barrier = pltpu.get_barrier_semaphore()

    @pl.when(z > 0)
    def _():
        pl.semaphore_signal(barrier, inc=1, device_id={"tensor": z - 1}, device_id_type=MESH)

    @pl.when(z < n - 1)
    def _():
        pl.semaphore_signal(barrier, inc=1, device_id={"tensor": z + 1}, device_id_type=MESH)

    for step in range(1, workers):
        pl.semaphore_signal(
            barrier, inc=1, device_id={"dp": lax.rem(worker + step, workers)}, device_id_type=MESH
        )

    places = (z, n - 1 - z)

    def named(way, index):
        return index if way == 0 else n - 1 - index

    def block(index):
        return pl.ds(pl.multiple_of(index * rows, rows), rows)

    def columns(j):
        return pl.ds(pl.multiple_of(j * width, width), width)

    def hop(way, j, k, src, dst):
        return pltpu.make_async_remote_copy(
            src_ref=src,
            dst_ref=dst,
            send_sem=send_sem.at[way, j, k],
            recv_sem=recv_sem.at[way, j, k],
            device_id={"tensor": z + 1 if way == 0 else z - 1},
            device_id_type=MESH,
        )

    def any_hop(way, j, k):
        return hop(way, j, k, last_sum.at[j], last_sum.at[j])

    def term(j, d):
        return lax.dot_general(
            cot_ref[block(d), :], w_ref[columns(j), :],
            (((1,), (1,)), ((), ())), preferred_element_type=jnp.float32,
        )

    def send_tokens(way, j, k, shard):
        piece = gathered.at[j, block(shard)]
        hop(way, j, k, piece, piece).start()

    def mask_own(j):
        gathered[j, block(z)] = (
            tok_ref[:, columns(j)].astype(jnp.float32) * mask_ref[...]
        ).astype(jnp.bfloat16)

    def send_own(j):
        for way in range(2):
            @pl.when(places[way] < n - 1)
            def _():
                send_tokens(way, j, 0, z)

    def slot(j, k):
        for way in range(2):
            place = places[way]

            @pl.when(place > 0)
            def _():
                any_hop(way, j, k).wait_recv()

            @pl.when(jnp.logical_and(k + 1 <= place, place < n - 1))
            def _():
                send_tokens(way, j, k + 1, named(way, place - 1 - k))

            @pl.when(k + 1 > place)
            def _():
                d = named(way, n + place - k - 1)
                total[...] = term(j, d)

                @pl.when(place > 0)
                def _():
                    total[...] += sums[j, d].astype(jnp.float32)

                sums[j, d] = total[...].astype(jnp.bfloat16)
                src = sums.at[j, d]
                dst = last_sum.at[j] if way == 1 and k + 1 == n - 1 else src
                hop(way, j, k + 1, src, dst).start()

    def vote_copy(j, step, source):
        piece = votes.at[source, j]
        return pltpu.make_async_remote_copy(
            src_ref=piece,
            dst_ref=piece,
            send_sem=vote_send.at[step, j],
            recv_sem=vote_recv.at[step, j],
            device_id={"dp": lax.rem(worker + step, workers)},
            device_id_type=MESH,
        )

    def momentum_step(j):
        def part(i, carry):
            at = pl.ds(pl.multiple_of(j * width + i * sub, sub), sub)
            key_grad = lax.dot_general(
                gathered[j, :, pl.ds(pl.multiple_of(i * sub, sub), sub)], cot_ref[...],
                (((0,), (0,)), ((), ())), preferred_element_type=jnp.float32,
            )
            prior = mom_ref[at, :].astype(jnp.float32)
            mom_out[at, :] = (beta_slow * prior + (1.0 - beta_slow) * key_grad).astype(jnp.bfloat16)
            interp = beta_vote * prior + (1.0 - beta_vote) * key_grad
            positive = (interp > 0).astype(jnp.int32)
            packed = positive[:words]
            for bit in range(1, 32):
                packed = packed | (positive[bit * words : (bit + 1) * words] << bit)
            votes[worker, j, pl.ds(pl.multiple_of(i * words, words), words)] = packed
            return carry

        lax.fori_loop(0, width // sub, part, 0)
        for step in range(1, workers):
            vote_copy(j, step, worker).start()

    def weight_step(j):
        for step in range(1, workers):
            vote_copy(j, step, worker).wait_recv()

        def part(i, carry):
            held = [
                votes[r, j, pl.ds(pl.multiple_of(i * words, words), words)] for r in range(workers)
            ]
            directions = []
            for bit in range(32):
                count = sum(((h >> bit) & 1) for h in held)
                twice = 2 * count - workers
                directions.append(jnp.minimum(jnp.maximum(twice, -1), 1))
            direction = jnp.concatenate(directions, 0).astype(jnp.float32)
            at = pl.ds(pl.multiple_of(j * width + i * sub, sub), sub)
            upd_out[at, :] = (w_ref[at, :].astype(jnp.float32) - step_rate * direction).astype(
                jnp.bfloat16
            )
            return carry

        lax.fori_loop(0, width // sub, part, 0)

    def finish_grad(j):
        total[...] = term(j, z)
        for way in range(2):
            @pl.when(places[way] > 0)
            def _():
                any_hop(way, j, n - 1).wait_recv()
                came = sums[j, z] if way == 0 else last_sum[j]
                total[...] += came.astype(jnp.float32)

        grad_out[:, columns(j)] = (total[...] * mask_ref[...]).astype(jnp.bfloat16)

    def each(function, start, end):
        def one(j, carry):
            function(j)
            return carry

        lax.fori_loop(start, end, one, 0)

    square = (rows, rows)
    diagonal = lax.broadcasted_iota(jnp.int32, square, 0) == lax.broadcasted_iota(
        jnp.int32, square, 1
    )
    spread = jnp.broadcast_to(mask_in[...].astype(jnp.float32), square)
    mask_ref[...] = jnp.sum(jnp.where(diagonal, spread, 0.0), axis=1, keepdims=True)
    loads[0].wait()
    each(mask_own, 0, lanes)

    @pl.when(jnp.logical_and(z > 0, z < n - 1))
    def _():
        pl.semaphore_wait(barrier, workers + 1)

    @pl.when(jnp.logical_or(z == 0, z == n - 1))
    def _():
        pl.semaphore_wait(barrier, workers)

    each(send_own, 0, lanes)

    def next_own(j):
        mask_own(j)
        send_own(j)

    def odd_last_slot(j):
        slot(j, n - 2)
        pl.when(lax.rem(j, 2) == 1)(lambda: momentum_step(j))

    def finish(j):
        pl.when(lax.rem(j, 2) == 0)(lambda: momentum_step(j))
        finish_grad(j)
        pl.when(j > 0)(lambda: weight_step(j - 1))

    each(next_own, lanes, chunks)
    for load in loads[1:]:
        load.wait()
    for k in range(n - 2):
        each(lambda j: slot(j, k), 0, chunks)
    each(odd_last_slot, 0, chunks)
    each(finish, 0, chunks)
    weight_step(chunks - 1)

    def drain(j, carry):
        for way in range(2):
            @pl.when(places[way] < n - 1)
            def _():
                for k in range(n):
                    any_hop(way, j, k).wait_send()
        for step in range(1, workers):
            vote_copy(j, step, worker).wait_send()
        return carry

    lax.fori_loop(0, chunks, drain, 0)


def store_kernel(pieces, *refs):
    count = len(refs) // 2
    sem = refs[-1]
    copies = []
    for source, target in zip(refs[:count], refs[count : 2 * count]):
        step = source.shape[0] // pieces
        for piece in range(pieces):
            at = pl.ds(piece * step, step)
            copies.append(
                pltpu.make_async_copy(source.at[at], target.at[at], sem.at[len(copies)])
            )
    for copy in copies:
        copy.start()
    for copy in copies:
        copy.wait()


def stored(*arrays):
    pieces = 2
    return pl.pallas_call(
        functools.partial(store_kernel, pieces),
        out_shape=tuple(jax.ShapeDtypeStruct(a.shape, a.dtype) for a in arrays),
        in_specs=[pl.BlockSpec(memory_space=pltpu.VMEM)] * len(arrays),
        out_specs=tuple(pl.BlockSpec(memory_space=pl.ANY) for _ in arrays),
        scratch_shapes=[pltpu.SemaphoreType.DMA((pieces * len(arrays),))],
        compiler_params=pltpu.CompilerParams(vmem_limit_bytes=16 * 2**20),
    )(*arrays)


def per_device(tokens_in, key_cot, row_mask, w_key, momentum):
    rows, features = tokens_in.shape
    head_cols = w_key.shape[1]
    n = lax.axis_size("tensor")
    workers = lax.axis_size("dp")
    sub = 256
    chunks = 10
    lanes = 2
    width = features // chunks
    bf16 = jnp.bfloat16
    vmem = pl.BlockSpec(memory_space=pltpu.VMEM)
    hbm = pl.BlockSpec(memory_space=pl.ANY)
    dma = pltpu.SemaphoreType.DMA
    input_grad, new_momentum, updated = pl.pallas_call(
        functools.partial(line_kernel, n, workers, chunks, lanes, sub),
        out_shape=(
            pltpu.VMEM((rows, features), bf16),
            pltpu.VMEM((features, head_cols), bf16),
            pltpu.VMEM((features, head_cols), bf16),
        ),
        in_specs=[hbm, hbm, vmem, hbm, hbm],
        out_specs=(vmem, vmem, vmem),
        scratch_shapes=[
            pltpu.VMEM((rows, features), bf16),
            pltpu.VMEM(key_cot.shape, bf16),
            pltpu.VMEM((features, head_cols), bf16),
            pltpu.VMEM((features, head_cols), bf16),
            pltpu.VMEM((rows, 1), jnp.float32),
            pltpu.VMEM((chunks, n * rows, width), bf16),
            pltpu.VMEM((chunks, n, rows, width), bf16),
            pltpu.VMEM((chunks, rows, width), bf16),
            pltpu.VMEM((rows, width), jnp.float32),
            pltpu.VMEM((workers, chunks, width // 32, head_cols), jnp.int32),
            dma((2, chunks, n)),
            dma((2, chunks, n)),
            dma((workers, chunks)),
            dma((workers, chunks)),
            dma((4,)),
        ],
        compiler_params=pltpu.CompilerParams(
            collective_id=0, has_side_effects=True, vmem_limit_bytes=56 * 2**20
        ),
        cost_estimate=pl.CostEstimate(
            flops=4 * n * rows * features * head_cols,
            bytes_accessed=2 * (2 * rows * features + 4 * features * head_cols),
            transcendentals=0,
        ),
    )(tokens_in, key_cot, row_mask[None], w_key, momentum[0])
    input_grad, new_momentum, updated = stored(input_grad, new_momentum, updated)
    column_block = updated
    position = lax.axis_index("tensor")
    for depth_bit in range((n // 4).bit_length() - 1):
        partner = swapped(column_block, "tensor", depth_bit)
        lower_half = jnp.bitwise_and(jnp.right_shift(position, depth_bit), 1) == 0
        column_block = jnp.where(
            lower_half,
            jnp.concatenate([column_block, partner], 1),
            jnp.concatenate([partner, column_block], 1),
        )
    return (input_grad, new_momentum[None], column_block[None])


def solution(mesh):
    return jax.shard_map(
        per_device,
        mesh=mesh,
        in_specs=(
            P(("section", "dp", "tensor"), None),
            P(("section", "dp"), "tensor"),
            P(("section", "dp", "tensor")),
            P("section", "tensor"),
            P("dp", "section", "tensor"),
        ),
        out_specs=(
            P(("section", "dp", "tensor"), None),
            P("dp", "section", "tensor"),
            P("tensor", "section", None),
        ),
        check_vma=False,
    )
```
